32 devices in a mesh: member: 2 (over x), lon: 8 (over z, y), lat: 2 (over core).
Axes of the slice: x: 2, y: 2, z: 4, core: 2. Of those that a mesh axis runs over, the one named last changes fastest.
Arguments:
- state: float32 [128, 256, 640], P(('member', 'lat'), 'lon'), parts along dimension 0, may hold values from -6 to 6
- dep_shift: int32 [2, 128, 256], P(None, ('member', 'lat'), 'lon'), parts along dimension 1, may hold values from -8 to 8, as said below
- dep_frac: float32 [2, 128, 256], P(None, ('member', 'lat'), 'lon'), parts along dimension 1, may hold values from 0 to 1
- stiff: float32 [640], replicated, may hold values from 0.05 to 0.2
Outputs:
- advanced: float32 [128, 256, 640], P(('member', 'lat'), 'lon'), parts along dimension 0
The draws below stay inside these ranges and needn't reach their ends.
There are 2 independent parts, one for each index of `member`. The reference program is written for one: setup_inputs(seed, part) draws one part's arguments, and reference() takes and returns one part's arrays. A program takes and returns all parts, laid end to end along the dimension named above; an argument that names none is the same for every part. Nothing has to cross between parts.
Inputs may be any that keep to these rules, and one draw needn't show every extreme that they name: `dep_shift`: both ends of the range are taken in every draw; the spread of displacements differs from row to row.
All inputs are finite; a program needn't handle non-finite values.
Results may differ from the reference program's by a relative error of at most 0.00007.
Values sent between devices are 32-bit elements; how exact they have to be, the bound alone decides.
No kernel may reach another device: no remote copies, remote signals or barrier semaphores. Data moves between devices by JAX's collectives and lax.ppermute only.
A program may use at most 64 MiB of HBM per device.

```python
import math
import jax
import jax.numpy as jnp

FIELDS = 5
LEV = 128
TRAJ = 2
REACH = 8
FL = 640
NLAT = 64
NLON = 256


def draw_dep_shift(key, part):
    first = jax.random.fold_in(key, 11)
    second = jax.random.fold_in(key, 23)
    speed = jax.random.randint(first, (TRAJ, NLAT, 1), 1, REACH + 1)
    raw = jax.random.randint(second, (TRAJ, NLAT, NLON), 0 - REACH, REACH + 1)
    shift = jnp.clip(raw, -speed, speed)
    shift = shift.at[:, 0, 0].set(0 - REACH)
    shift = shift.at[:, -1, -1].set(REACH)
    return shift.astype(jnp.int32)


def block_scale(key, extent, shards, least, high):
    gain, own = 1.0, jax.random.fold_in(key, 6)
    for dim, shards_of in shards:
        draws = jnp.exp(jax.random.uniform(jax.random.fold_in(own, dim), (shards_of,), jnp.float32, least / len(shards), high / len(shards)))
        gain = gain * jnp.repeat(draws, extent[dim] // shards_of).reshape([-1 if axis == dim else 1 for axis in range(len(extent))])
    return gain


def centred(own_key, extent, spread, reach, split=(), kind=jnp.bfloat16):
    entries = spread * jax.random.normal(own_key, extent, jnp.float32)
    if split:
        entries = entries * block_scale(own_key, extent, split, -0.22, 0.18)
    return jnp.clip(entries, -reach, reach).astype(kind)


def setup_inputs(seed: int = 0, part: int = 0) -> dict:
    seeds = jax.random.split(jax.random.key(seed), 5)
    part_splits = jax.random.split(jax.random.fold_in(seeds[4], part), 5)
    state = centred(part_splits[0], (NLAT, NLON, FL), 1.0, 6.0, ((0, 2), (1, 8)), jnp.float32)
    dep_shift = draw_dep_shift(jax.random.fold_in(jax.random.fold_in(seeds[4], part), 71), part)
    dep_frac = jnp.clip(1.0 * jax.random.uniform(part_splits[2], (TRAJ, NLAT, NLON), jnp.float32) ** block_scale(part_splits[2], (TRAJ, NLAT, NLON), ((1, 2), (2, 8)), -0.2, 0.2), 0.0, 1.0)
    stiff = jnp.clip(jnp.exp(jax.random.uniform(seeds[3], (FL,), jnp.float32, math.log(0.05), math.log(0.2))), 0.05, 0.2)
    return {"state": state, "dep_shift": dep_shift, "dep_frac": dep_frac, "stiff": stiff}


OMEGAS = (0.4227, 0.8104)


def vertical(rows, frac):
    shaped = rows.reshape(rows.shape[:-1] + (FIELDS, LEV))
    upper = jnp.concatenate([shaped[..., 1:], shaped[..., -1:]], axis=-1)
    mixed = shaped + frac[..., None, None] * (upper - shaped)
    return mixed.reshape(rows.shape)


def sweep(field, rhs, stiff, omega):
    east = jnp.roll(field, -1, axis=1)
    west = jnp.roll(field, 1, axis=1)
    blank = jnp.zeros_like(field[:1])
    north = jnp.concatenate([field[1:], blank], axis=0)
    south = jnp.concatenate([blank, field[:-1]], axis=0)
    lap = ((south + north) + (west + east)) - 4.0 * field
    resid = rhs - (field - stiff * lap)
    return field + omega * resid


def reference(state, dep_shift, dep_frac, stiff):
    lon_index = jnp.arange(NLON, dtype=jnp.int32)[None, :]
    field = state
    for turn in range(TRAJ):
        src_lon = (lon_index + dep_shift[turn]) % NLON
        upstream = jnp.take_along_axis(state, src_lon[:, :, None].astype(jnp.int32), axis=1)
        rhs = vertical(upstream, dep_frac[turn])
        for which in range(2):
            field = sweep(field, rhs, stiff, OMEGAS[which])
    return field
```

```python
import functools

import jax
import jax.numpy as jnp
from jax import lax
from jax.experimental import pallas as pl
from jax.experimental.pallas import tpu as pltpu
from jax.sharding import PartitionSpec as P

LEV = 128
TRAJ = 2
REACH = 8
OMEGAS = (0.4227, 0.8104)

NEAR = 2 * TRAJ
FAR = REACH - 1
SLOTS = 80
LANES = 128
SIDE = 16
UP_ROWS = 4
SWEEP_ROWS = 6


def ring(axis, step):
    count = lax.axis_size(axis)
    return [(i, (i + step) % count) for i in range(count)]


def pairs(axis, start):
    count = lax.axis_size(axis)
    edges = [(i, (i + 1) % count) for i in range(start, count, 2)]
    return edges + [(b, a) for a, b in edges]


def start_kernel(
    info_ref,
    shift_ref,
    frac_ref,
    state_ref,
    own_ref,
    edge_ref,
    left_a_ref,
    left_b_ref,
    right_a_ref,
    right_b_ref,
    pad,
    sides,
    sems,
):
    turns, rows, cols = shift_ref.shape
    edge_row = jnp.where(info_ref[0] == 0, rows - NEAR, 0)
    fetch = [
        pltpu.make_async_copy(state_ref.at[:, pl.ds(0, 8), :], sides.at[0], sems.at[0]),
        pltpu.make_async_copy(state_ref.at[:, pl.ds(cols - 8, 8), :], sides.at[1], sems.at[1]),
        pltpu.make_async_copy(state_ref.at[pl.ds(edge_row, NEAR)], edge_ref, sems.at[2]),
    ]
    for copy in fetch:
        copy.start()
    pad[...] = jnp.zeros_like(pad)
    for kind in range(2 * turns):
        value = shift_ref[kind].astype(jnp.float32) if kind < turns else frac_ref[kind - turns]
        pad[0:rows, 0:cols] = value
        own_ref[kind] = jnp.transpose(pad[...])[0:cols, :]
    half = left_a_ref.shape[0] // NEAR
    for side, (first, refs) in enumerate(((0, (left_a_ref, left_b_ref)), (8 - NEAR, (right_a_ref, right_b_ref)))):
        fetch[side].wait()
        for r in range(0, rows, 2):
            two = jnp.concatenate([sides[side, r + v, first : first + NEAR, :] for v in range(2)], axis=0)
            n = r % half * NEAR
            refs[r // half][n : n + 2 * NEAR, :] = two
    fetch[2].wait()


def second_kernel(
    info_ref,
    own_ref,
    next_ref,
    edge_ref,
    left_ref,
    right_ref,
    to_left_ref,
    to_right_ref,
    more_left_ref,
    more_right_ref,
    dep_ref,
    *,
    rows,
):
    kinds, cols, _ = own_ref.shape
    low = info_ref[0] == 0
    lat_rows = rows - NEAR
    lane = lax.broadcasted_iota(jnp.int32, (cols, LANES), 1)
    head = jnp.zeros((8, to_left_ref.shape[1]), jnp.float32)
    to_left_ref[...] = head
    to_right_ref[...] = head
    for kind in range(kinds):
        own, other = own_ref[kind], next_ref[kind]
        other = jnp.where(low, pltpu.roll(other, lat_rows, 1), pltpu.roll(other, NEAR, 1))
        both = jnp.where(lane < lat_rows, own, other)
        dep_ref[kind] = both
        to_left_ref[0:NEAR, kind * LANES : (kind + 1) * LANES] = both[0:NEAR, :]
        to_right_ref[0:NEAR, kind * LANES : (kind + 1) * LANES] = both[cols - NEAR : cols, :]
    count = left_ref.shape[0]
    more_left_ref[0:count, :] = left_ref[...]
    more_right_ref[0:count, :] = right_ref[...]
    for r in range(NEAR):
        more_left_ref[count + r * NEAR : count + r * NEAR + NEAR, :] = edge_ref[r, 0:NEAR, :]
        more_right_ref[count + r * NEAR : count + r * NEAR + NEAR, :] = edge_ref[r, cols - NEAR : cols, :]


def list_slots(bits_ref, which, rows, cols, firsts, list_ref, slots):
    def row(m, counts):
        low, high = counts
        base = m * cols
        low_bits, high_bits = bits_ref[which, m], bits_ref[which + 1, m]
        for j in range(FAR):
            list_ref[0, jnp.minimum(low, slots)] = base + (firsts[0][0] + firsts[0][1] * j)
            list_ref[1, jnp.minimum(high, slots)] = base + (firsts[1][0] + firsts[1][1] * j)
            low = low + ((low_bits >> j) & 1)
            high = high + ((high_bits >> j) & 1)
        return low, high

    low, high = lax.fori_loop(0, rows, row, (jnp.int32(0), jnp.int32(0)))
    list_ref[0, slots + 1] = low
    list_ref[1, slots + 1] = high


def pack_kernel(
    info_ref,
    dep_ref,
    state_ref,
    edge_ref,
    from_left_ref,
    from_right_ref,
    low_ref,
    high_ref,
    flags,
    wide_ref,
    buf,
    heads,
    bits,
    lists,
    sems,
    *,
    rows,
    slots,
):
    kinds, cols, _ = dep_ref.shape
    wide = cols + 2 * NEAR
    lat_rows = rows - NEAR
    low = info_ref[0] == 0
    own, extra = lat_rows * cols, NEAR * cols
    fetch = [
        pltpu.make_async_copy(from_left_ref, heads.at[0], sems.at[0]),
        pltpu.make_async_copy(from_right_ref, heads.at[1], sems.at[1]),
        pltpu.make_async_copy(state_ref, buf.at[pl.ds(0, own)], sems.at[2]),
        pltpu.make_async_copy(edge_ref, buf.at[pl.ds(own, extra)], sems.at[3]),
    ]
    for copy in fetch:
        copy.start()

    def clear(n, _):
        for side in range(2):
            lists[side, n] = 0
        return 0

    lax.fori_loop(0, slots + 1, clear, 0)
    fetch[0].wait()
    fetch[1].wait()
    for kind in range(kinds):
        lanes = slice(kind * LANES, (kind + 1) * LANES)
        wide_ref[kind, 0:NEAR, :] = heads[0, 0:NEAR, lanes]
        wide_ref[kind, NEAR : NEAR + cols, :] = dep_ref[kind]
        wide_ref[kind, NEAR + cols : wide, :] = heads[1, 0:NEAR, lanes]

    lane = lax.broadcasted_iota(jnp.int32, (1, LANES), 1)
    beyond = jnp.where(low, lane - lat_rows + 1, rows - lane)
    beyond = jnp.where(lane < lat_rows, 0, jnp.where(lane < rows, beyond, rows))
    reach = [NEAR - 1 - 2 * turn for turn in range(TRAJ)]
    groups = (
        ([0] * TRAJ, 0, 1),
        ([cols + NEAR - r for r in reach], cols - 1, -1),
        ([NEAR - r for r in reach], -1, -1),
        ([cols] * TRAJ, cols, 1),
    )
    for which, (first, anchor, sign) in enumerate(groups):
        total = jnp.zeros((1, LANES), jnp.int32)
        hits = [jnp.zeros((1, LANES), bool) for _ in range(FAR)]
        for turn in range(TRAJ):
            for q in range(first[turn], first[turn] + NEAR + reach[turn]):
                target = wide_ref[turn, q : q + 1, :].astype(jnp.int32) + (q - NEAR)
                target = jnp.where(beyond <= reach[turn], target, -4 * LANES)
                for j in range(FAR):
                    hits[j] = hits[j] | (target == anchor + sign * (NEAR + j))
        for j in range(FAR):
            total = total + jnp.where(hits[j], 1 << j, 0)
        flags[which : which + 1, :] = total
    flags[len(groups) : 8, :] = jnp.zeros((8 - len(groups), LANES), jnp.int32)
    copy = pltpu.make_async_copy(flags, bits, sems.at[4])
    copy.start()
    copy.wait()

    list_slots(bits, 0, rows, cols, ((NEAR, 1), (cols - 1 - NEAR, -1)), lists, slots)
    fetch[2].wait()
    fetch[3].wait()

    def gather(group, _):
        for u in range(8):
            n = group * 8 + u
            low_ref[pl.ds(n, 1), :] = buf[pl.ds(lists[0, n], 1), :]
            high_ref[pl.ds(n, 1), :] = buf[pl.ds(lists[1, n], 1), :]
        return 0

    lax.fori_loop(0, slots // 8, gather, 0)


def weights_kernel(bits_ref, wide_ref, pick_ref, frac_ref, taken, counts, sent, *, rows, slots):
    kinds, wide, _ = wide_ref.shape
    cols = wide - 2 * NEAR
    list_slots(bits_ref, 2, rows, LANES, ((SIDE - 1 - NEAR, -1), (SIDE + cols + NEAR, 1)), taken, slots)
    list_slots(bits_ref, 0, rows, LANES, ((0, 0), (0, 0)), sent, slots)
    for side in range(2):
        counts[side] = jnp.maximum(taken[side, slots + 1], sent[side, slots + 1])
    groups, band = wide // 8, wide - 2 * NEAR + 2 * SIDE
    place = lax.broadcasted_iota(jnp.int32, (8, LANES), 1)
    place = jnp.where(place < band, place, place - band).astype(jnp.float32)
    column = lax.broadcasted_iota(jnp.int32, (8, LANES), 0) * groups + (SIDE - NEAR)
    for turn in range(TRAJ):
        for k in range(groups):
            target = wide_ref[turn, pl.ds(k, 8, stride=groups), :] + (column + k).astype(jnp.float32)
            frac = wide_ref[TRAJ + turn, pl.ds(k, 8, stride=groups), :]
            at = slice(turn * wide + 8 * k, turn * wide + 8 * k + 8)
            for m in range(rows):
                pick_ref[m, at, :] = jnp.where(target[:, m : m + 1] == place, 1.0, 0.0)
                frac_ref[m, at, :] = jnp.broadcast_to(frac[:, m : m + 1], (8, LANES))


def main_kernel(
    rows,
    cols,
    slots,
    info_ref,
    lists_ref,
    state_ref,
    edge_ref,
    low_a_ref,
    low_b_ref,
    high_a_ref,
    high_b_ref,
    far_low_ref,
    far_high_ref,
    full_ref,
    counts_ref,
    pick_any,
    frac_any,
    stiff_ref,
    out_any,
    out_ref,
    full,
    ext,
    rhs,
    xa,
    xb,
    nat,
    pick_ref,
    frac_ref,
    sems,
):
    lat_rows = state_ref.shape[0]
    tiles = state_ref.shape[2] // LEV
    wide = cols + 2 * NEAR
    groups = wide // 8
    own0 = jnp.where(info_ref[0] == 0, 0, NEAR)
    ext0 = jnp.where(info_ref[0] == 0, lat_rows, 0)
    copies = []
    for f in range(tiles):
        lanes = pl.ds(f * LEV, LEV)
        copies.append(
            pltpu.make_async_copy(
                state_ref.at[:, :, lanes],
                ext.at[f, pl.ds(own0, lat_rows), pl.ds(SIDE, cols), :],
                sems.at[f],
            )
        )
        copies[-1].start()
        copies.append(
            pltpu.make_async_copy(
                edge_ref.at[:, :, lanes],
                ext.at[f, pl.ds(ext0, NEAR), pl.ds(SIDE, cols), :],
                sems.at[tiles + f],
            )
        )
        copies[-1].start()
    copies.append(pltpu.make_async_copy(pick_any, pick_ref, sems.at[2 * tiles]))
    copies.append(pltpu.make_async_copy(frac_any, frac_ref, sems.at[2 * tiles + 1]))
    copies[-2].start()
    copies[-1].start()

    zero = jnp.zeros((8, LEV), jnp.float32)

    def clear(e, _):
        for f in range(tiles):
            for start in (0, 8, SIDE + cols, SIDE + cols + 8):
                ext[f, e, start : start + 8, :] = zero
        return 0

    lax.fori_loop(0, rows, clear, 0)
    for f in range(tiles):
        for start in range(0, SIDE * 2 + cols, 8):
            ext[f, rows, start : start + 8, :] = zero
        for k in range(groups):
            xa[f, rows, 8 * k : 8 * k + 8, :] = zero
            xb[f, rows, 8 * k : 8 * k + 8, :] = zero
    half = low_a_ref.shape[0] // NEAR

    def near(m, base, refs):
        e = jnp.where(m < lat_rows, own0 + m, ext0 + m - lat_rows)
        start = pl.multiple_of(base, 8)
        for ref, col in zip(refs, (SIDE - NEAR, SIDE + cols)):
            two = ref[pl.ds(start, 2 * NEAR), :]
            for f in range(tiles):
                for v in range(2):
                    ext[f, e + v, col : col + NEAR, :] = two[v * NEAR : (v + 1) * NEAR, f * LEV : (f + 1) * LEV]

    def near_a(group, _):
        near(2 * group, group * 8, (low_a_ref, high_a_ref))
        return 0

    def near_b(group, _):
        near(half + 2 * group, group * 8, (low_b_ref, high_b_ref))
        return 0

    lax.fori_loop(0, half // 2, near_a, 0)
    lax.fori_loop(0, (rows - half) // 2, near_b, 0)
    for side, far_ref in enumerate((far_low_ref, far_high_ref)):

        def put(m, col, column):
            e = jnp.where(m < lat_rows, own0 + m, ext0 + m - lat_rows)
            for f in range(tiles):
                ext[f, e, pl.ds(col, 1), :] = column[:, f * LEV : (f + 1) * LEV]

        @pl.when(counts_ref[side] <= slots)
        def _(side=side, far_ref=far_ref, put=put):
            def place(n, _):
                address = lists_ref[side, n]
                put(address >> 7, address & (LANES - 1), far_ref[pl.ds(n, 1), :])
                return 0

            lax.fori_loop(0, lists_ref[side, slots + 1], place, 0)

        @pl.when(counts_ref[side] > slots)
        def _(side=side, put=put):
            copy = pltpu.make_async_copy(full_ref.at[side], full, sems.at[2 * tiles + 2])
            copy.start()
            copy.wait()
            first_col = (SIDE - NEAR - FAR, SIDE + cols + NEAR)[side]

            def place(m, _):
                for j in range(FAR):
                    put(m, first_col + j, full[pl.ds(m * FAR + j, 1), :])
                return 0

            lax.fori_loop(0, rows, place, 0)

    for copy in copies:
        copy.wait()

    top = lax.broadcasted_iota(jnp.int32, (wide, LEV), 1) == LEV - 1

    def upstream(group, _):
        for v in range(UP_ROWS):
            e = group * UP_ROWS + v
            his, los = [], []
            for f in range(tiles):
                value = ext[f, e]
                hi = value.astype(jnp.bfloat16)
                his.append(hi)
                los.append((value - hi.astype(jnp.float32)).astype(jnp.bfloat16))
            band = jnp.concatenate([jnp.concatenate(his, axis=1), jnp.concatenate(los, axis=1)], axis=0)
            own = (e >= own0) & (e < own0 + lat_rows)
            m = jnp.where(own, e - own0, e - ext0 + lat_rows)
            got = jnp.dot(pick_ref[m].astype(jnp.bfloat16), band, preferred_element_type=jnp.float32)
            for turn in range(TRAJ):
                frac = frac_ref[m, turn * wide : (turn + 1) * wide, :]
                for f in range(tiles):
                    u = got[turn * wide : (turn + 1) * wide, f * LEV : (f + 1) * LEV]
                    up = jnp.where(top, u, pltpu.roll(u, LEV - 1, 1))
                    rhs[turn, f, e] = u + frac * (up - u)
        return 0

    lax.fori_loop(0, rows // UP_ROWS, upstream, 0)

    def tile(f, _):
        s = stiff_ref[f]
        prev = 1.0
        for sweep in range(2 * TRAJ):
            omega = OMEGAS[sweep % 2]
            alpha = jnp.broadcast_to((1.0 - omega - 4.0 * omega * s) * (prev / omega), (8, LEV))
            beta = jnp.broadcast_to(s * prev, (8, LEV))
            prev = omega
            turn = sweep // 2
            src, dst = (None, xa, xb, xa)[sweep], (xa, xb, xa, None)[sweep]

            def load(e, src=src):
                if src is None:
                    return [ext[f, e, pl.ds(SIDE - NEAR + k, 8, stride=groups), :] for k in range(groups)]
                return [src[f, e, 8 * k : 8 * k + 8, :] for k in range(groups)]

            def block(group, carry, load=load, dst=dst, alpha=alpha, beta=beta, turn=turn, omega=omega):
                south, mid = carry
                for v in range(SWEEP_ROWS):
                    e = group * SWEEP_ROWS + v
                    north = load(e + 1)
                    for k in range(groups):
                        west = mid[k - 1] if k else pltpu.roll(mid[groups - 1], 1, 0)
                        east = mid[k + 1] if k < groups - 1 else pltpu.roll(mid[0], 7, 0)
                        around = (south[k] + north[k]) + (west + east)
                        new = alpha * mid[k] + beta * around + rhs[turn, f, e, 8 * k : 8 * k + 8, :]
                        if dst is None:
                            nat[e, pl.ds(k, 8, stride=groups), :] = new * omega
                        else:
                            dst[f, e, 8 * k : 8 * k + 8, :] = new
                    south, mid = mid, north
                return south, mid

            lax.fori_loop(0, rows // SWEEP_ROWS, block, ([zero] * groups, load(0)))

        for r in range(lat_rows):
            out_ref[f, r] = nat[own0 + r, NEAR : NEAR + cols, :]
        lanes = pl.ds(pl.multiple_of(f * LEV, LEV), LEV)
        pltpu.make_async_copy(out_ref.at[f], out_any.at[:, :, lanes], sems.at[f]).start()
        return 0

    lax.fori_loop(0, tiles, tile, 0)
    for f in range(tiles):
        pltpu.make_async_copy(out_ref.at[f], out_any.at[:, :, pl.ds(f * LEV, LEV)], sems.at[f]).wait()


def shards(state, dep_shift, dep_frac, stiff):
    lat_rows, cols, width = state.shape
    tiles = width // LEV
    rows = lat_rows + NEAR
    wide = cols + 2 * NEAR
    band = cols + 2 * SIDE
    kinds = 2 * TRAJ
    lat = lax.axis_index("lat")
    low = lat == 0
    right, left = ring("lon", 1), ring("lon", -1)
    swap = ring("lat", 1)
    info = lat[None]
    shape = functools.partial(jax.ShapeDtypeStruct, dtype=jnp.float32)
    smem = pl.BlockSpec(memory_space=pltpu.SMEM)
    vmem = pl.BlockSpec(memory_space=pltpu.VMEM)
    anywhere = pl.BlockSpec(memory_space=pl.ANY)

    half = shape((lat_rows // 2 * NEAR, width))
    own, edge, left_a, left_b, right_a, right_b = pl.pallas_call(
        start_kernel,
        out_shape=(shape((kinds, cols, LANES)), shape((NEAR, cols, width)), half, half, half, half),
        in_specs=[smem, vmem, vmem, anywhere],
        out_specs=(vmem,) * 6,
        scratch_shapes=[
            pltpu.VMEM((LANES, LANES), jnp.float32),
            pltpu.VMEM((2, lat_rows, 8, width), jnp.float32),
            pltpu.SemaphoreType.DMA((3,)),
        ],
        compiler_params=pltpu.CompilerParams(vmem_limit_bytes=16 * 2**20),
    )(info, dep_shift, dep_frac, state)
    other = lax.ppermute(own, "lat", swap)
    edge = lax.ppermute(edge, "lat", swap)
    low_a = lax.ppermute(right_a, "lon", right)
    high_a = lax.ppermute(left_a, "lon", left)
    head = shape((8, width))
    more = shape((half.shape[0] + NEAR * NEAR, width))
    to_left, to_right, left_b, right_b, dep = pl.pallas_call(
        functools.partial(second_kernel, rows=rows),
        out_shape=(head, head, more, more, shape((kinds, cols, LANES))),
        in_specs=[smem] + [vmem] * 5,
        out_specs=(vmem,) * 5,
    )(info, own, other, edge, left_b, right_b)
    from_left = lax.ppermute(to_right, "lon", right)
    from_right = lax.ppermute(to_left, "lon", left)
    low_b = lax.ppermute(right_b, "lon", right)
    high_b = lax.ppermute(left_b, "lon", left)

    message = shape((SLOTS, width))
    send_low, send_high, flags, around = pl.pallas_call(
        functools.partial(pack_kernel, rows=rows, slots=SLOTS),
        out_shape=(message, message, jax.ShapeDtypeStruct((8, LANES), jnp.int32), shape((kinds, wide, LANES))),
        in_specs=[smem, vmem] + [anywhere] * 4,
        out_specs=(vmem,) * 4,
        scratch_shapes=[
            pltpu.VMEM((rows * cols, width), jnp.float32),
            pltpu.VMEM((2, 8, width), jnp.float32),
            pltpu.SMEM((8, LANES), jnp.int32),
            pltpu.SMEM((2, SLOTS + 8), jnp.int32),
            pltpu.SemaphoreType.DMA((5,)),
        ],
        compiler_params=pltpu.CompilerParams(vmem_limit_bytes=16 * 2**20),
        cost_estimate=pl.CostEstimate(flops=0, bytes_accessed=4 * 2**20, transcendentals=0),
    )(info, dep, state.reshape(lat_rows * cols, width), edge.reshape(NEAR * cols, width), from_left, from_right)
    far_high = lax.ppermute(send_low, "lon", left)
    far_low = lax.ppermute(send_high, "lon", right)

    pick, frac, taken, counts = pl.pallas_call(
        functools.partial(weights_kernel, rows=rows, slots=SLOTS),
        out_shape=(
            shape((rows, TRAJ * wide, LANES)),
            shape((rows, TRAJ * wide, LANES)),
            jax.ShapeDtypeStruct((2, SLOTS + 8), jnp.int32),
            jax.ShapeDtypeStruct((2,), jnp.int32),
        ),
        in_specs=[smem, vmem],
        out_specs=(vmem, vmem, smem, smem),
        scratch_shapes=[pltpu.SMEM((2, SLOTS + 8), jnp.int32)],
        compiler_params=pltpu.CompilerParams(vmem_limit_bytes=16 * 2**20),
    )(flags, around)

    over_left, over_right = counts[0] > SLOTS, counts[1] > SLOTS
    size = -(-rows * FAR // 8) * 8
    nothing = jnp.zeros((size, width), jnp.float32)

    def whole():
        field = jnp.concatenate([state, edge], axis=0)
        pad = ((0, size - rows * FAR), (0, 0))
        at_left = jnp.pad(field[:, NEAR : NEAR + FAR].reshape(rows * FAR, width), pad)
        at_right = jnp.pad(field[:, cols - NEAR - FAR : cols - NEAR].reshape(rows * FAR, width), pad)
        even = lax.axis_index("lon") % 2 == 0
        got_even = lax.cond(
            jnp.where(even, over_right, over_left),
            lambda: lax.ppermute(jnp.where(even, at_right, at_left), "lon", pairs("lon", 0)),
            lambda: nothing,
        )
        got_odd = lax.cond(
            jnp.where(even, over_left, over_right),
            lambda: lax.ppermute(jnp.where(even, at_left, at_right), "lon", pairs("lon", 1)),
            lambda: nothing,
        )
        return jnp.where(even, jnp.stack([got_odd, got_even]), jnp.stack([got_even, got_odd]))

    full = lax.cond(over_left | over_right, whole, lambda: jnp.stack([nothing, nothing]))

    return pl.pallas_call(
        functools.partial(main_kernel, rows, cols, SLOTS),
        out_shape=shape(state.shape),
        in_specs=[smem, smem, anywhere, anywhere] + [vmem] * 6 + [anywhere, smem] + [anywhere] * 2 + [vmem],
        out_specs=anywhere,
        scratch_shapes=[
            pltpu.VMEM((tiles, lat_rows, cols, LEV), jnp.float32),
            pltpu.VMEM((size, width), jnp.float32),
            pltpu.VMEM((tiles, rows + 1, band, LEV), jnp.float32),
            pltpu.VMEM((TRAJ, tiles, rows, wide, LEV), jnp.float32),
            pltpu.VMEM((tiles, rows + 1, wide, LEV), jnp.float32),
            pltpu.VMEM((tiles, rows + 1, wide, LEV), jnp.float32),
            pltpu.VMEM((rows, wide, LEV), jnp.float32),
            pltpu.VMEM((rows, TRAJ * wide, LANES), jnp.float32),
            pltpu.VMEM((rows, TRAJ * wide, LANES), jnp.float32),
            pltpu.SemaphoreType.DMA((2 * tiles + 3,)),
        ],
        compiler_params=pltpu.CompilerParams(vmem_limit_bytes=40 * 2**20),
        cost_estimate=pl.CostEstimate(flops=200_000_000, bytes_accessed=8 * 2**20, transcendentals=0),
    )(
        info, taken, state, edge, low_a, low_b, high_a, high_b, far_low, far_high, full, counts, pick, frac,
        stiff.reshape(tiles, 1, LEV),
    )


def solution(mesh):
    in_specs = (
        P(("member", "lat"), "lon", None),
        P(None, ("member", "lat"), "lon"),
        P(None, ("member", "lat"), "lon"),
        P(),
    )
    out_specs = P(("member", "lat"), "lon", None)
    return jax.shard_map(shards, mesh=mesh, in_specs=in_specs, out_specs=out_specs, check_vma=False)
```

```python
import functools

import jax
import jax.numpy as jnp
from jax import lax
from jax.experimental import pallas as pl
from jax.experimental.pallas import tpu as pltpu
from jax.sharding import PartitionSpec as P

LEV = 128
TRAJ = 2
REACH = 8
OMEGAS = (0.4227, 0.8104)

NEAR = 2 * TRAJ
FAR = REACH - 1
SLOTS = 80
LANES = 128
SIDE = 16
UP_ROWS = 4
SWEEP_ROWS = 6


def ring(axis, step):
    count = lax.axis_size(axis)
    return [(i, (i + step) % count) for i in range(count)]


def pairs(axis, start):
    count = lax.axis_size(axis)
    edges = [(i, (i + 1) % count) for i in range(start, count, 2)]
    return edges + [(b, a) for a, b in edges]


def start_kernel(
    info_ref,
    shift_ref,
    frac_ref,
    state_ref,
    own_ref,
    edge_ref,
    left_ref,
    right_ref,
    shift,
    frac,
    pad,
    sides,
    sems,
):
    turns, rows, cols = shift_ref.shape
    edge_row = jnp.where(info_ref[0] == 0, rows - NEAR, 0)
    fetch = [
        pltpu.make_async_copy(state_ref.at[:, pl.ds(0, 8), :], sides.at[0], sems.at[0]),
        pltpu.make_async_copy(state_ref.at[:, pl.ds(cols - 8, 8), :], sides.at[1], sems.at[1]),
        pltpu.make_async_copy(state_ref.at[pl.ds(edge_row, NEAR)], edge_ref, sems.at[2]),
        pltpu.make_async_copy(shift_ref, shift, sems.at[3]),
        pltpu.make_async_copy(frac_ref, frac, sems.at[4]),
    ]
    for copy in reversed(fetch):
        copy.start()
    pad[...] = jnp.zeros_like(pad)
    fetch[3].wait()
    fetch[4].wait()
    for kind in range(2 * turns):
        value = shift[kind].astype(jnp.float32) if kind < turns else frac[kind - turns]
        pad[0:rows, 0:cols] = value
        own_ref[kind] = jnp.transpose(pad[...])[0:cols, :]
    for side, (first, ref) in enumerate(((0, left_ref), (8 - NEAR, right_ref))):
        fetch[side].wait()
        for r in range(0, rows, 2):
            two = jnp.concatenate([sides[side, r + v, first : first + NEAR, :] for v in range(2)], axis=0)
            ref[r * NEAR : (r + 2) * NEAR, :] = two
    fetch[2].wait()


def second_kernel(
    info_ref,
    own_ref,
    next_ref,
    edge_ref,
    left_ref,
    right_ref,
    left_a_ref,
    right_a_ref,
    left_b_ref,
    right_b_ref,
    dep_ref,
    *,
    rows,
):
    kinds, cols, _ = own_ref.shape
    low = info_ref[0] == 0
    lat_rows = rows - NEAR
    lane = lax.broadcasted_iota(jnp.int32, (cols, LANES), 1)
    head = jnp.zeros((8, left_ref.shape[1]), jnp.float32)
    left_a_ref[0:8, :] = head
    right_a_ref[0:8, :] = head
    for kind in range(kinds):
        own, other = own_ref[kind], next_ref[kind]
        other = jnp.where(low, pltpu.roll(other, lat_rows, 1), pltpu.roll(other, NEAR, 1))
        both = jnp.where(lane < lat_rows, own, other)
        dep_ref[kind] = both
        left_a_ref[0:NEAR, kind * LANES : (kind + 1) * LANES] = both[0:NEAR, :]
        right_a_ref[0:NEAR, kind * LANES : (kind + 1) * LANES] = both[cols - NEAR : cols, :]
    some = left_a_ref.shape[0] - 8
    rest = lat_rows * NEAR - some
    left_a_ref[8 : 8 + some, :] = left_ref[0:some, :]
    right_a_ref[8 : 8 + some, :] = right_ref[0:some, :]
    left_b_ref[0:rest, :] = left_ref[some : some + rest, :]
    right_b_ref[0:rest, :] = right_ref[some : some + rest, :]
    for r in range(NEAR):
        at = slice(rest + r * NEAR, rest + (r + 1) * NEAR)
        left_b_ref[at, :] = edge_ref[r, 0:NEAR, :]
        right_b_ref[at, :] = edge_ref[r, cols - NEAR : cols, :]


def list_slots(bits_ref, which, rows, cols, firsts, list_ref):
    def row(m, counts):
        low, high = counts
        base = m * cols
        low_bits, high_bits = bits_ref[which, m], bits_ref[which + 1, m]
        for j in range(FAR):
            list_ref[0, low] = base + (firsts[0][0] + firsts[0][1] * j)
            list_ref[1, high] = base + (firsts[1][0] + firsts[1][1] * j)
            low = low + ((low_bits >> j) & 1)
            high = high + ((high_bits >> j) & 1)
        return low, high

    return lax.fori_loop(0, rows, row, (jnp.int32(0), jnp.int32(0)))


def pack_kernel(
    info_ref,
    dep_ref,
    state_ref,
    edge_ref,
    from_left_ref,
    from_right_ref,
    low_ref,
    high_ref,
    flags,
    sent,
    wide_ref,
    buf,
    heads,
    bits,
    lists,
    sems,
    *,
    rows,
    slots,
):
    kinds, cols, _ = dep_ref.shape
    wide = cols + 2 * NEAR
    lat_rows = rows - NEAR
    low = info_ref[0] == 0
    own, extra = lat_rows * cols, NEAR * cols
    fetch = [
        pltpu.make_async_copy(from_left_ref.at[pl.ds(0, 8)], heads.at[0], sems.at[0]),
        pltpu.make_async_copy(from_right_ref.at[pl.ds(0, 8)], heads.at[1], sems.at[1]),
        pltpu.make_async_copy(state_ref, buf.at[pl.ds(0, own)], sems.at[2]),
        pltpu.make_async_copy(edge_ref, buf.at[pl.ds(own, extra)], sems.at[3]),
    ]
    for copy in fetch:
        copy.start()

    def clear(n, _):
        for side in range(2):
            lists[side, n] = 0
        return 0

    lax.fori_loop(0, slots + 1, clear, 0)
    fetch[0].wait()
    fetch[1].wait()
    for kind in range(kinds):
        lanes = slice(kind * LANES, (kind + 1) * LANES)
        wide_ref[kind, 0:NEAR, :] = heads[0, 0:NEAR, lanes]
        wide_ref[kind, NEAR : NEAR + cols, :] = dep_ref[kind]
        wide_ref[kind, NEAR + cols : wide, :] = heads[1, 0:NEAR, lanes]

    lane = lax.broadcasted_iota(jnp.int32, (1, LANES), 1)
    beyond = jnp.where(low, lane - lat_rows + 1, rows - lane)
    beyond = jnp.where(lane < lat_rows, 0, jnp.where(lane < rows, beyond, rows))
    reach = [NEAR - 1 - 2 * turn for turn in range(TRAJ)]
    groups = (
        ([0] * TRAJ, 0, 1),
        ([cols + NEAR - r for r in reach], cols - 1, -1),
        ([NEAR - r for r in reach], -1, -1),
        ([cols] * TRAJ, cols, 1),
    )
    flags[...] = jnp.zeros_like(flags)
    for which, (first, anchor, sign) in enumerate(groups):
        total = jnp.zeros((1, LANES), jnp.int32)
        for turn in range(TRAJ):
            for q in range(first[turn], first[turn] + NEAR + reach[turn]):
                target = wide_ref[turn, q : q + 1, :].astype(jnp.int32) + (q - NEAR)
                j = sign * (target - anchor) - NEAR
                hit = (j >= 0) & (j < FAR) & (beyond <= reach[turn])
                total = total | jnp.where(hit, jnp.left_shift(1, jnp.maximum(j, 0)), 0)
        flags[which : which + 1, :] = total
    copy = pltpu.make_async_copy(flags, bits, sems.at[4])
    copy.start()
    copy.wait()

    sent[0], sent[1] = list_slots(bits, 0, rows, cols, ((NEAR, 1), (cols - 1 - NEAR, -1)), lists)
    fetch[2].wait()
    fetch[3].wait()

    def gather(group, _):
        for u in range(8):
            n = group * 8 + u
            low_ref[pl.ds(n, 1), :] = buf[pl.ds(lists[0, n], 1), :]
            high_ref[pl.ds(n, 1), :] = buf[pl.ds(lists[1, n], 1), :]
        return 0

    lax.fori_loop(0, slots // 8, gather, 0)


def weights_kernel(bits_ref, sent_ref, wide_ref, _, pick_ref, frac_ref, taken, counts, over, *, rows, slots):
    kinds, wide, _ = wide_ref.shape
    cols = wide - 2 * NEAR
    got = list_slots(bits_ref, 2, rows, LANES, ((SIDE - 1 - NEAR, -1), (SIDE + cols + NEAR, 1)), taken)
    for side in range(2):
        counts[side] = got[side]
        counts[2 + side] = jnp.maximum(got[side], sent_ref[side])
    over[0] = (jnp.maximum(counts[2], counts[3]) > slots).astype(jnp.int32)
    groups, band = wide // 8, wide - 2 * NEAR + 2 * SIDE
    place = lax.broadcasted_iota(jnp.int32, (8, LANES), 1)
    place = jnp.where(place < band, place, place - band).astype(jnp.float32)
    column = lax.broadcasted_iota(jnp.int32, (8, LANES), 0) * groups + (SIDE - NEAR)
    for turn in range(TRAJ):
        for k in range(groups):
            target = wide_ref[turn, pl.ds(k, 8, stride=groups), :] + (column + k).astype(jnp.float32)
            frac = wide_ref[TRAJ + turn, pl.ds(k, 8, stride=groups), :]
            at = slice(turn * wide + 8 * k, turn * wide + 8 * k + 8)
            for m in range(rows):
                pick_ref[m, at, :] = jnp.where(target[:, m : m + 1] == place, 1.0, 0.0)
                frac_ref[m, at, :] = jnp.broadcast_to(frac[:, m : m + 1], (8, LANES))


def main_kernel(
    rows,
    cols,
    slots,
    info_ref,
    lists_ref,
    state_ref,
    edge_ref,
    low_a_ref,
    low_b_ref,
    high_a_ref,
    high_b_ref,
    far_low_ref,
    far_high_ref,
    full_ref,
    counts_ref,
    pick_any,
    frac_any,
    stiff_ref,
    out_any,
    out_ref,
    full,
    ext,
    rhs,
    xa,
    xb,
    nat,
    pick_ref,
    frac_ref,
    sems,
):
    lat_rows = state_ref.shape[0]
    tiles = state_ref.shape[2] // LEV
    wide = cols + 2 * NEAR
    groups = wide // 8
    own0 = jnp.where(info_ref[0] == 0, 0, NEAR)
    ext0 = jnp.where(info_ref[0] == 0, lat_rows, 0)
    copies = []
    for f in range(tiles):
        lanes = pl.ds(f * LEV, LEV)
        copies.append(
            pltpu.make_async_copy(
                state_ref.at[:, :, lanes],
                ext.at[f, pl.ds(own0, lat_rows), pl.ds(SIDE, cols), :],
                sems.at[f],
            )
        )
        copies[-1].start()
        copies.append(
            pltpu.make_async_copy(
                edge_ref.at[:, :, lanes],
                ext.at[f, pl.ds(ext0, NEAR), pl.ds(SIDE, cols), :],
                sems.at[tiles + f],
            )
        )
        copies[-1].start()
    copies.append(pltpu.make_async_copy(pick_any, pick_ref, sems.at[2 * tiles]))
    copies.append(pltpu.make_async_copy(frac_any, frac_ref, sems.at[2 * tiles + 1]))
    copies[-2].start()
    copies[-1].start()

    zero = jnp.zeros((8, LEV), jnp.float32)

    def clear(e, _):
        for f in range(tiles):
            for start in (0, 8, SIDE + cols, SIDE + cols + 8):
                ext[f, e, start : start + 8, :] = zero
        return 0

    lax.fori_loop(0, rows, clear, 0)
    for f in range(tiles):
        for start in range(0, SIDE * 2 + cols, 8):
            ext[f, rows, start : start + 8, :] = zero
        for k in range(groups):
            xa[f, rows, 8 * k : 8 * k + 8, :] = zero
            xb[f, rows, 8 * k : 8 * k + 8, :] = zero
    half = (low_a_ref.shape[0] - 8) // NEAR

    def near(m, base, refs):
        e = jnp.where(m < lat_rows, own0 + m, ext0 + m - lat_rows)
        start = pl.multiple_of(base, 8)
        for ref, col in zip(refs, (SIDE - NEAR, SIDE + cols)):
            two = ref[pl.ds(start, 2 * NEAR), :]
            for f in range(tiles):
                for v in range(2):
                    ext[f, e + v, col : col + NEAR, :] = two[v * NEAR : (v + 1) * NEAR, f * LEV : (f + 1) * LEV]

    def near_a(group, _):
        near(2 * group, 8 + group * 8, (low_a_ref, high_a_ref))
        return 0

    def near_b(group, _):
        near(half + 2 * group, group * 8, (low_b_ref, high_b_ref))
        return 0

    lax.fori_loop(0, half // 2, near_a, 0)
    lax.fori_loop(0, (rows - half) // 2, near_b, 0)
    for side, far_ref in enumerate((far_low_ref, far_high_ref)):

        def put(m, col, column):
            e = jnp.where(m < lat_rows, own0 + m, ext0 + m - lat_rows)
            for f in range(tiles):
                ext[f, e, pl.ds(col, 1), :] = column[:, f * LEV : (f + 1) * LEV]

        @pl.when(counts_ref[2 + side] <= slots)
        def _(side=side, far_ref=far_ref, put=put):
            def place(n, _):
                address = lists_ref[side, n]
                put(address >> 7, address & (LANES - 1), far_ref[pl.ds(n, 1), :])
                return 0

            lax.fori_loop(0, counts_ref[side], place, 0)

        @pl.when(counts_ref[2 + side] > slots)
        def _(side=side, put=put):
            copy = pltpu.make_async_copy(full_ref.at[side], full, sems.at[2 * tiles + 2])
            copy.start()
            copy.wait()
            first_col = (SIDE - NEAR - FAR, SIDE + cols + NEAR)[side]

            def place(m, _):
                for j in range(FAR):
                    put(m, first_col + j, full[pl.ds(m * FAR + j, 1), :])
                return 0

            lax.fori_loop(0, rows, place, 0)

    for copy in copies:
        copy.wait()

    top = lax.broadcasted_iota(jnp.int32, (wide, LEV), 1) == LEV - 1

    def upstream(group, _):
        for v in range(UP_ROWS):
            e = group * UP_ROWS + v
            his, los = [], []
            for f in range(tiles):
                value = ext[f, e]
                hi = value.astype(jnp.bfloat16)
                his.append(hi)
                los.append((value - hi.astype(jnp.float32)).astype(jnp.bfloat16))
            band = jnp.concatenate([jnp.concatenate(his, axis=1), jnp.concatenate(los, axis=1)], axis=0)
            own = (e >= own0) & (e < own0 + lat_rows)
            m = jnp.where(own, e - own0, e - ext0 + lat_rows)
            got = jnp.dot(pick_ref[m].astype(jnp.bfloat16), band, preferred_element_type=jnp.float32)
            for turn in range(TRAJ):
                frac = frac_ref[m, turn * wide : (turn + 1) * wide, :]
                for f in range(tiles):
                    u = got[turn * wide : (turn + 1) * wide, f * LEV : (f + 1) * LEV]
                    up = jnp.where(top, u, pltpu.roll(u, LEV - 1, 1))
                    rhs[turn, f, e] = u + frac * (up - u)
        return 0

    lax.fori_loop(0, rows // UP_ROWS, upstream, 0)

    def tile(f, _):
        s = stiff_ref[f]
        prev = 1.0
        for sweep in range(2 * TRAJ):
            omega = OMEGAS[sweep % 2]
            alpha = jnp.broadcast_to((1.0 - omega - 4.0 * omega * s) * (prev / omega), (8, LEV))
            beta = jnp.broadcast_to(s * prev, (8, LEV))
            prev = omega
            turn = sweep // 2
            src, dst = (None, xa, xb, xa)[sweep], (xa, xb, xa, None)[sweep]

            def load(e, src=src):
                if src is None:
                    return [ext[f, e, pl.ds(SIDE - NEAR + k, 8, stride=groups), :] for k in range(groups)]
                return [src[f, e, 8 * k : 8 * k + 8, :] for k in range(groups)]

            def block(group, carry, load=load, dst=dst, alpha=alpha, beta=beta, turn=turn, omega=omega):
                south, mid = carry
                for v in range(SWEEP_ROWS):
                    e = group * SWEEP_ROWS + v
                    north = load(e + 1)
                    for k in range(groups):
                        west = mid[k - 1] if k else pltpu.roll(mid[groups - 1], 1, 0)
                        east = mid[k + 1] if k < groups - 1 else pltpu.roll(mid[0], 7, 0)
                        around = (south[k] + north[k]) + (west + east)
                        new = alpha * mid[k] + beta * around + rhs[turn, f, e, 8 * k : 8 * k + 8, :]
                        if dst is None:
                            nat[e, pl.ds(k, 8, stride=groups), :] = new * omega
                        else:
                            dst[f, e, 8 * k : 8 * k + 8, :] = new
                    south, mid = mid, north
                return south, mid

            lax.fori_loop(0, rows // SWEEP_ROWS, block, ([zero] * groups, load(0)))

        for r in range(lat_rows):
            out_ref[f, r] = nat[own0 + r, NEAR : NEAR + cols, :]
        lanes = pl.ds(pl.multiple_of(f * LEV, LEV), LEV)
        pltpu.make_async_copy(out_ref.at[f], out_any.at[:, :, lanes], sems.at[f]).start()
        return 0

    lax.fori_loop(0, tiles, tile, 0)
    for f in range(tiles):
        pltpu.make_async_copy(out_ref.at[f], out_any.at[:, :, pl.ds(f * LEV, LEV)], sems.at[f]).wait()


def shards(state, dep_shift, dep_frac, stiff):
    lat_rows, cols, width = state.shape
    tiles = width // LEV
    rows = lat_rows + NEAR
    wide = cols + 2 * NEAR
    band = cols + 2 * SIDE
    kinds = 2 * TRAJ
    lat = lax.axis_index("lat")
    low = lat == 0
    right, left = ring("lon", 1), ring("lon", -1)
    swap = ring("lat", 1)
    info = lat[None]
    shape = functools.partial(jax.ShapeDtypeStruct, dtype=jnp.float32)
    smem = pl.BlockSpec(memory_space=pltpu.SMEM)
    vmem = pl.BlockSpec(memory_space=pltpu.VMEM)
    anywhere = pl.BlockSpec(memory_space=pl.ANY)
    hbm = pl.BlockSpec(memory_space=pltpu.HBM)

    near = shape((lat_rows * NEAR, width))
    own, edge, near_left, near_right = pl.pallas_call(
        start_kernel,
        out_shape=(shape((kinds, cols, LANES)), shape((NEAR, cols, width)), near, near),
        in_specs=[smem] + [hbm] * 3,
        out_specs=(vmem,) * 4,
        scratch_shapes=[
            pltpu.VMEM(dep_shift.shape, jnp.int32),
            pltpu.VMEM(dep_frac.shape, jnp.float32),
            pltpu.VMEM((LANES, LANES), jnp.float32),
            pltpu.VMEM((2, lat_rows, 8, width), jnp.float32),
            pltpu.SemaphoreType.DMA((5,)),
        ],
        compiler_params=pltpu.CompilerParams(vmem_limit_bytes=16 * 2**20),
    )(info, dep_shift, dep_frac, state)
    other = lax.ppermute(own, "lat", swap)
    edge = lax.ppermute(edge, "lat", swap)
    some = lat_rows // 4 * NEAR
    first = shape((8 + some, width))
    second = shape((lat_rows * NEAR - some + NEAR * NEAR, width))
    left_a, right_a, left_b, right_b, dep = pl.pallas_call(
        functools.partial(second_kernel, rows=rows),
        out_shape=(first, first, second, second, shape((kinds, cols, LANES))),
        in_specs=[smem] + [vmem] * 5,
        out_specs=(vmem,) * 5,
        compiler_params=pltpu.CompilerParams(vmem_limit_bytes=4 * 2**20),
    )(info, own, other, edge, near_left, near_right)
    low_a = lax.ppermute(right_a, "lon", right)
    high_a = lax.ppermute(left_a, "lon", left)
    low_b = lax.ppermute(right_b, "lon", right)
    high_b = lax.ppermute(left_b, "lon", left)

    message = shape((SLOTS, width))
    size = -(-rows * FAR // 8) * 8
    send_low, send_high, flags, sent, around = pl.pallas_call(
        functools.partial(pack_kernel, rows=rows, slots=SLOTS),
        out_shape=(
            message,
            message,
            jax.ShapeDtypeStruct((8, LANES), jnp.int32),
            jax.ShapeDtypeStruct((2,), jnp.int32),
            shape((kinds, wide, LANES)),
        ),
        in_specs=[smem, vmem] + [anywhere] * 4,
        out_specs=(vmem, vmem, vmem, smem, vmem),
        scratch_shapes=[
            pltpu.VMEM((rows * cols, width), jnp.float32),
            pltpu.VMEM((2, 8, width), jnp.float32),
            pltpu.SMEM((8, LANES), jnp.int32),
            pltpu.SMEM((2, size + 8), jnp.int32),
            pltpu.SemaphoreType.DMA((5,)),
        ],
        compiler_params=pltpu.CompilerParams(vmem_limit_bytes=16 * 2**20),
        cost_estimate=pl.CostEstimate(flops=0, bytes_accessed=4 * 2**20, transcendentals=0),
    )(info, dep, state.reshape(lat_rows * cols, width), edge.reshape(NEAR * cols, width), low_a, high_a)
    far_high = lax.ppermute(send_low, "lon", left)
    far_low = lax.ppermute(send_high, "lon", right)

    pick, frac, taken, counts, over = pl.pallas_call(
        functools.partial(weights_kernel, rows=rows, slots=SLOTS),
        out_shape=(
            shape((rows, TRAJ * wide, LANES)),
            shape((rows, TRAJ * wide, LANES)),
            jax.ShapeDtypeStruct((2, size + 8), jnp.int32),
            jax.ShapeDtypeStruct((4,), jnp.int32),
            jax.ShapeDtypeStruct((1,), jnp.int32),
        ),
        in_specs=[smem, smem, vmem, anywhere],
        out_specs=(vmem, vmem, smem, smem, smem),
        compiler_params=pltpu.CompilerParams(vmem_limit_bytes=16 * 2**20),
    )(flags, sent, around, low_b)

    nothing = jnp.zeros((size, width), jnp.float32)

    def whole():
        over_left, over_right = counts[2] > SLOTS, counts[3] > SLOTS
        field = jnp.concatenate([state, edge], axis=0)
        pad = ((0, size - rows * FAR), (0, 0))
        at_left = jnp.pad(field[:, NEAR : NEAR + FAR].reshape(rows * FAR, width), pad)
        at_right = jnp.pad(field[:, cols - NEAR - FAR : cols - NEAR].reshape(rows * FAR, width), pad)
        even = lax.axis_index("lon") % 2 == 0
        got_even = lax.cond(
            jnp.where(even, over_right, over_left),
            lambda: lax.ppermute(jnp.where(even, at_right, at_left), "lon", pairs("lon", 0)),
            lambda: nothing,
        )
        got_odd = lax.cond(
            jnp.where(even, over_left, over_right),
            lambda: lax.ppermute(jnp.where(even, at_left, at_right), "lon", pairs("lon", 1)),
            lambda: nothing,
        )
        return jnp.where(even, jnp.stack([got_odd, got_even]), jnp.stack([got_even, got_odd]))

    full = lax.cond(over[0] > 0, whole, lambda: jnp.stack([nothing, nothing]))

    return pl.pallas_call(
        functools.partial(main_kernel, rows, cols, SLOTS),
        out_shape=shape(state.shape),
        in_specs=[smem, smem, anywhere, anywhere] + [vmem] * 6 + [anywhere, smem] + [anywhere] * 2 + [vmem],
        out_specs=anywhere,
        scratch_shapes=[
            pltpu.VMEM((tiles, lat_rows, cols, LEV), jnp.float32),
            pltpu.VMEM((size, width), jnp.float32),
            pltpu.VMEM((tiles, rows + 1, band, LEV), jnp.float32),
            pltpu.VMEM((TRAJ, tiles, rows, wide, LEV), jnp.float32),
            pltpu.VMEM((tiles, rows + 1, wide, LEV), jnp.float32),
            pltpu.VMEM((tiles, rows + 1, wide, LEV), jnp.float32),
            pltpu.VMEM((rows, wide, LEV), jnp.float32),
            pltpu.VMEM((rows, TRAJ * wide, LANES), jnp.float32),
            pltpu.VMEM((rows, TRAJ * wide, LANES), jnp.float32),
            pltpu.SemaphoreType.DMA((2 * tiles + 3,)),
        ],
        compiler_params=pltpu.CompilerParams(vmem_limit_bytes=40 * 2**20),
        cost_estimate=pl.CostEstimate(flops=200_000_000, bytes_accessed=8 * 2**20, transcendentals=0),
    )(
        info, taken, state, edge, low_a, low_b, high_a, high_b, far_low, far_high, full, counts, pick, frac,
        stiff.reshape(tiles, 1, LEV),
    )


def solution(mesh):
    in_specs = (
        P(("member", "lat"), "lon", None),
        P(None, ("member", "lat"), "lon"),
        P(None, ("member", "lat"), "lon"),
        P(),
    )
    out_specs = P(("member", "lat"), "lon", None)
    return jax.shard_map(shards, mesh=mesh, in_specs=in_specs, out_specs=out_specs, check_vma=False)
```

```python
import functools

import jax
import jax.numpy as jnp
from jax import lax
from jax.experimental import pallas as pl
from jax.experimental.pallas import tpu as pltpu
from jax.sharding import PartitionSpec as P

LEV = 128
TRAJ = 2
REACH = 8
OMEGAS = (0.4227, 0.8104)

NEAR = 2 * TRAJ
FAR = REACH - 1
SLOTS = 80
LANES = 128
SIDE = 8
UP_ROWS = 6
SWEEP_ROWS = 6


def ring(axis, step):
    count = lax.axis_size(axis)
    return [(i, (i + step) % count) for i in range(count)]


def pairs(axis, start):
    count = lax.axis_size(axis)
    edges = [(i, (i + 1) % count) for i in range(start, count, 2)]
    return edges + [(b, a) for a, b in edges]


def start_kernel(
    info_ref,
    dep_ref,
    state_ref,
    own_ref,
    edge_ref,
    left_ref,
    right_ref,
    pad,
    sides,
    sems,
):
    kinds, rows, cols = dep_ref.shape
    edge_row = jnp.where(info_ref[0] == 0, rows - NEAR, 0)
    fetch = [
        pltpu.make_async_copy(state_ref.at[:, pl.ds(0, 8), :], sides.at[0], sems.at[0]),
        pltpu.make_async_copy(state_ref.at[:, pl.ds(cols - 8, 8), :], sides.at[1], sems.at[1]),
        pltpu.make_async_copy(state_ref.at[pl.ds(edge_row, NEAR)], edge_ref, sems.at[2]),
    ]
    for copy in fetch:
        copy.start()
    pad[...] = jnp.zeros_like(pad)
    for kind in range(kinds):
        pad[0:rows, 0:cols] = dep_ref[kind]
        own_ref[kind] = jnp.transpose(pad[...])[0:cols, :]
    for side, (first, ref) in enumerate(((0, left_ref), (8 - NEAR, right_ref))):
        fetch[side].wait()
        for r in range(0, rows, 2):
            two = jnp.concatenate([sides[side, r + v, first : first + NEAR, :] for v in range(2)], axis=0)
            ref[r * NEAR : (r + 2) * NEAR, :] = two
    fetch[2].wait()


def second_kernel(
    info_ref,
    own_ref,
    next_ref,
    edge_ref,
    left_ref,
    right_ref,
    left_a_ref,
    right_a_ref,
    left_b_ref,
    right_b_ref,
    dep_ref,
    *,
    rows,
):
    kinds, cols, _ = own_ref.shape
    low = info_ref[0] == 0
    lat_rows = rows - NEAR
    lane = lax.broadcasted_iota(jnp.int32, (cols, LANES), 1)
    head = jnp.zeros((8, left_ref.shape[1]), jnp.float32)
    left_a_ref[0:8, :] = head
    right_a_ref[0:8, :] = head
    for kind in range(kinds):
        own, other = own_ref[kind], next_ref[kind]
        other = jnp.where(low, pltpu.roll(other, lat_rows, 1), pltpu.roll(other, NEAR, 1))
        both = jnp.where(lane < lat_rows, own, other)
        dep_ref[kind] = both
        left_a_ref[0:NEAR, kind * LANES : (kind + 1) * LANES] = both[0:NEAR, :]
        right_a_ref[0:NEAR, kind * LANES : (kind + 1) * LANES] = both[cols - NEAR : cols, :]
    some = left_a_ref.shape[0] - 8
    rest = lat_rows * NEAR - some
    left_a_ref[8 : 8 + some, :] = left_ref[0:some, :]
    right_a_ref[8 : 8 + some, :] = right_ref[0:some, :]
    left_b_ref[0:rest, :] = left_ref[some : some + rest, :]
    right_b_ref[0:rest, :] = right_ref[some : some + rest, :]
    for r in range(NEAR):
        at = slice(rest + r * NEAR, rest + (r + 1) * NEAR)
        left_b_ref[at, :] = edge_ref[r, 0:NEAR, :]
        right_b_ref[at, :] = edge_ref[r, cols - NEAR : cols, :]


def pack_kernel(
    info_ref,
    dep_ref,
    state_ref,
    edge_ref,
    from_left_ref,
    from_right_ref,
    low_ref,
    high_ref,
    notes_ref,
    over,
    wide_ref,
    notes,
    sem,
    *,
    rows,
    slots,
):
    kinds, cols, _ = dep_ref.shape
    wide = cols + 2 * NEAR
    lat_rows = rows - NEAR
    low = info_ref[0] == 0
    for kind in range(kinds):
        lanes = slice(kind * LANES, (kind + 1) * LANES)
        wide_ref[kind, 0:NEAR, :] = from_left_ref[0:NEAR, lanes]
        wide_ref[kind, NEAR : NEAR + cols, :] = dep_ref[kind]
        wide_ref[kind, NEAR + cols : wide, :] = from_right_ref[0:NEAR, lanes]

    lane = lax.broadcasted_iota(jnp.int32, (1, LANES), 1)
    beyond = jnp.where(low, lane - lat_rows + 1, rows - lane)
    beyond = jnp.where(lane < lat_rows, 0, jnp.where(lane < rows, beyond, rows))
    reach = [NEAR - 1 - 2 * turn for turn in range(TRAJ)]
    groups = (
        ([0] * TRAJ, 0, 1),
        ([cols + NEAR - r for r in reach], cols - 1, -1),
        ([NEAR - r for r in reach], -1, -1),
        ([cols] * TRAJ, cols, 1),
    )
    totals = []
    for first, anchor, sign in groups:
        total = jnp.zeros((1, LANES), jnp.int32)
        for turn in range(TRAJ):
            for q in range(first[turn], first[turn] + NEAR + reach[turn]):
                target = wide_ref[turn, q : q + 1, :].astype(jnp.int32) + (q - NEAR)
                j = sign * (target - anchor) - NEAR
                hit = (j >= 0) & (j < FAR) & (beyond <= reach[turn])
                total = total | jnp.where(hit, jnp.left_shift(1, jnp.maximum(j, 0)), 0)
        totals.append(total)
    totals = jnp.concatenate(totals + [jnp.zeros((8 - len(groups), LANES), jnp.int32)], axis=0)

    hits = [(totals >> j) & 1 for j in range(FAR)]
    in_row = sum(hits[1:], hits[0])
    upto, lanes8 = in_row, lax.broadcasted_iota(jnp.int32, (8, LANES), 1)
    for d in (1, 2, 4, 8, 16, 32, 64):
        upto = upto + jnp.where(lanes8 >= d, pltpu.roll(upto, d, 1), 0)
    place, places = upto - in_row, []
    for hit in hits:
        places.append(jnp.where(hit == 1, place, -1))
        place = place + hit
    n = lax.broadcasted_iota(jnp.int32, (slots, LANES), 0)
    diagonal = n == lax.broadcasted_iota(jnp.int32, (slots, LANES), 1)
    addresses = (
        (2, 8, 0, 1),
        (3, 8, 0, 1),
        (0, cols, NEAR, 1),
        (1, cols, cols - 1 - NEAR, -1),
    )
    notes_ref[0 : len(groups), :] = upto[0 : len(groups)]
    for i, (which, stride, first, sign) in enumerate(addresses):
        found = jnp.zeros((slots, LANES), jnp.float32)
        for j in range(FAR):
            address = (lane * stride + (first + sign * j)).astype(jnp.float32)
            found = found + jnp.where(places[j][which : which + 1] == n, address, 0.0)
        found = jnp.where(diagonal, jnp.sum(found, axis=1, keepdims=True), 0.0)
        notes_ref[len(groups) + i : len(groups) + i + 1, :] = jnp.sum(found, axis=0, keepdims=True).astype(jnp.int32)
    copy = pltpu.make_async_copy(notes_ref, notes, sem)
    copy.start()
    copy.wait()
    sent = [notes[side, LANES - 1] for side in range(2)]
    most = jnp.maximum(jnp.maximum(sent[0], sent[1]), jnp.maximum(notes[2, LANES - 1], notes[3, LANES - 1]))
    over[0] = (most > slots).astype(jnp.int32)
    own = lat_rows * cols

    def gather(group, _):
        for u in range(8):
            n = group * 8 + u
            for side, ref in enumerate((low_ref, high_ref)):
                address = jnp.minimum(notes[6 + side, n], own - 1)
                ref[pl.ds(n, 1), :] = state_ref[pl.ds(address, 1), :]
        return 0

    lax.fori_loop(0, slots // 8, gather, 0)

    def gather_edge(side, ref):
        def body(n):
            ref[pl.ds(n, 1), :] = edge_ref[pl.ds(notes[6 + side, n] - own, 1), :]
            return n - 1

        start = jnp.minimum(sent[side], slots) - 1
        lax.while_loop(lambda n: (n >= 0) & (notes[6 + side, jnp.maximum(n, 0)] >= own), body, start)

    gather_edge(0, low_ref)
    gather_edge(1, high_ref)


def arranged(ref, index, start, groups):
    middle = groups - 2
    parts = [ref[index + (pl.ds(start, 8), slice(None))]]
    parts += [ref[index + (pl.ds(start + 8 + k, 8, stride=middle), slice(None))] for k in range(middle)]
    return parts + [ref[index + (pl.ds(start + 8 * (groups - 1), 8), slice(None))]]


def weights_kernel(wide_ref, pick_ref, frac_ref, far_ref, kept_ref, sem, *, rows):
    kinds, wide, _ = wide_ref.shape
    cols = wide - 2 * NEAR
    keep = pltpu.make_async_copy(wide_ref, kept_ref, sem)
    keep.start()
    groups, band = wide // 8, cols + 2 * SIDE
    place = lax.broadcasted_iota(jnp.int32, (8, LANES), 1)
    place = jnp.where(place < band, place, place - band)
    place = jnp.where(place < band, place, -LANES).astype(jnp.float32)
    sub = lax.broadcasted_iota(jnp.int32, (8, LANES), 0)
    firsts = [sub] + [8 + k + sub * (groups - 2) for k in range(groups - 2)] + [8 * (groups - 1) + sub]
    parts = []
    for turn in range(TRAJ):
        for k, shift in enumerate(arranged(wide_ref, (turn,), 0, groups)):
            parts.append(shift + (firsts[k] - NEAR).astype(jnp.float32))
    fracs = [frac for turn in range(TRAJ) for frac in arranged(wide_ref, (TRAJ + turn,), 0, groups)]
    highs = [frac.astype(jnp.bfloat16).astype(jnp.float32) for frac in fracs]
    parts += highs + [frac - high for frac, high in zip(fracs, highs)]
    table = jnp.concatenate(parts, axis=0).astype(jnp.bfloat16)
    row = lax.broadcasted_iota(jnp.int32, (LANES, LANES), 0)
    count = TRAJ * wide
    for m in range(rows):
        spread = jnp.dot(table, jnp.where(row == m, 1.0, 0.0).astype(jnp.bfloat16), preferred_element_type=jnp.float32)
        frac_ref[m] = spread[count : 2 * count] + spread[2 * count :]
        for n in range(TRAJ * groups):
            column = spread[8 * n : 8 * n + 8]
            pick_ref[m, 8 * n : 8 * n + 8, :] = jnp.where(column + SIDE == place, 1.0, 0.0)
            turn, k = divmod(n, groups)
            if k == 0:
                far_ref[0, turn, m] = -1 - NEAR - column
            if k == groups - 1:
                far_ref[1, turn, m] = column - (cols + NEAR)
    keep.wait()


def gather_kernel(
    info_ref,
    state_ref,
    edge_ref,
    low_a_ref,
    high_a_ref,
    low_b_ref,
    high_b_ref,
    pick_ref,
    frac_ref,
    rhs,
    x_ref,
    *rest,
):
    *kept, ext, sems = rest
    lat_rows, cols, width = state_ref.shape
    tiles = width // LEV
    rows = lat_rows + NEAR
    wide = cols + 2 * NEAR
    groups, band = wide // 8, cols + 2 * SIDE
    own0 = jnp.where(info_ref[0] == 0, 0, NEAR)
    ext0 = jnp.where(info_ref[0] == 0, lat_rows, 0)
    copies = []
    for f in range(tiles):
        lanes = pl.ds(f * LEV, LEV)
        for i, (ref, first, count) in enumerate(((state_ref, own0, lat_rows), (edge_ref, ext0, NEAR))):
            copies.append(
                pltpu.make_async_copy(
                    ref.at[:, :, lanes],
                    ext.at[f, pl.ds(first, count), pl.ds(SIDE, cols), :],
                    sems.at[2 * f + i],
                )
            )
            copies[-1].start()
    keeps = []
    for i, (source, target) in enumerate(zip((edge_ref, low_a_ref, high_a_ref, low_b_ref, high_b_ref), kept)):
        keeps.append(pltpu.make_async_copy(source, target, sems.at[2 * tiles + i]))
        keeps[-1].start()
    zero = jnp.zeros((8, LEV), jnp.float32)
    for f in range(tiles):
        for k in range(groups):
            x_ref[f, rows, 8 * k : 8 * k + 8, :] = zero

    first = (low_a_ref.shape[0] - 8) // NEAR
    blank = jnp.zeros((SIDE - NEAR, LEV), jnp.float32)

    def near(m, start, low, high):
        e = jnp.where(m < lat_rows, own0 + m, ext0 + m - lat_rows)
        at = pl.ds(pl.multiple_of(start, 8), 2 * NEAR)
        west, east = low[at, :], high[at, :]
        for f in range(tiles):
            for v in range(2):
                part = (slice(v * NEAR, (v + 1) * NEAR), slice(f * LEV, (f + 1) * LEV))
                ext[f, e + v, 0:SIDE, :] = jnp.concatenate([blank, west[part]], axis=0)
                ext[f, e + v, SIDE + cols : band, :] = jnp.concatenate([east[part], blank], axis=0)

    def near_a(n, _):
        near(2 * n, 8 + 2 * NEAR * n, low_a_ref, high_a_ref)
        return 0

    def near_b(n, _):
        near(first + 2 * n, 2 * NEAR * n, low_b_ref, high_b_ref)
        return 0

    lax.fori_loop(0, first // 2, near_a, 0)
    lax.fori_loop(0, (rows - first) // 2, near_b, 0)
    for copy in copies:
        copy.wait()

    top = lax.broadcasted_iota(jnp.int32, (wide, LEV), 1) == LEV - 1

    def upstream(group, _):
        for v in range(UP_ROWS):
            e = group * UP_ROWS + v
            own = (e >= own0) & (e < own0 + lat_rows)
            m = jnp.where(own, e - own0, e - ext0 + lat_rows)
            his, los = [], []
            for f in range(tiles):
                value = ext[f, e]
                hi = value.astype(jnp.bfloat16)
                his.append(hi)
                los.append((value - hi.astype(jnp.float32)).astype(jnp.bfloat16))
                for k, part in enumerate(arranged(ext, (f, e), SIDE - NEAR, groups)):
                    x_ref[f, e, 8 * k : 8 * k + 8, :] = part
            field = jnp.concatenate([jnp.concatenate(his, axis=1), jnp.concatenate(los, axis=1)], axis=0)
            pick = pick_ref[m].astype(jnp.bfloat16)[:, : 2 * band]
            got = jnp.dot(pick, field, preferred_element_type=jnp.float32)
            for turn in range(TRAJ):
                frac = frac_ref[m, turn * wide : (turn + 1) * wide, :]
                for f in range(tiles):
                    u = got[turn * wide : (turn + 1) * wide, f * LEV : (f + 1) * LEV]
                    up = jnp.where(top, u, pltpu.roll(u, LEV - 1, 1))
                    rhs[turn, f, e] = u + frac * (up - u)
        return 0

    lax.fori_loop(0, rows // UP_ROWS, upstream, 0)
    for keep in keeps:
        keep.wait()


def main_kernel(
    info_ref,
    notes_ref,
    far_low_ref,
    far_high_ref,
    met_ref,
    frac_ref,
    stiff_ref,
    x_ref,
    rhs_in,
    out_any,
    rhs,
    low_kept,
    high_kept,
    ups,
    xa,
    xb,
    nat,
    sems,
    *,
    slots,
):
    lat_rows, cols, width = out_any.shape
    tiles = width // LEV
    rows = lat_rows + NEAR
    wide = cols + 2 * NEAR
    groups = wide // 8
    own0 = jnp.where(info_ref[0] == 0, 0, NEAR)
    ext0 = jnp.where(info_ref[0] == 0, lat_rows, 0)
    keeps = [
        pltpu.make_async_copy(far_low_ref, low_kept, sems.at[tiles]),
        pltpu.make_async_copy(far_high_ref, high_kept, sems.at[tiles + 1]),
    ]
    for keep in keeps:
        keep.start()
    zero = jnp.zeros((8, LEV), jnp.float32)
    for f in range(tiles):
        for k in range(groups):
            xa[f, rows, 8 * k : 8 * k + 8, :] = zero
            xb[f, rows, 8 * k : 8 * k + 8, :] = zero

    def lift(source, count):
        def block(n, _):
            at = pl.ds(pl.multiple_of(n * 8, 8), 8)
            lane = lax.broadcasted_iota(jnp.int32, (8, LEV), 1)
            for f in range(tiles):
                lanes = slice(f * LEV, (f + 1) * LEV)
                u = source[at, lanes]
                ups[at, lanes] = jnp.where(lane == LEV - 1, u, pltpu.roll(u, LEV - 1, 1))
            return 0

        lax.fori_loop(0, count // 8, block, 0)

    def put(side, m, j, source, n):
        k = 0 if side == 0 else groups - 1
        e = jnp.where(m < lat_rows, own0 + m, ext0 + m - lat_rows)
        column, up = source[pl.ds(n, 1), :], ups[pl.ds(n, 1), :]
        for turn in range(TRAJ):
            hit = met_ref[side, turn, m] == j.astype(jnp.float32)
            frac = frac_ref[m, turn * wide + 8 * k : turn * wide + 8 * k + 8, :]
            for f in range(tiles):
                u, v = column[:, f * LEV : (f + 1) * LEV], up[:, f * LEV : (f + 1) * LEV]
                mixed = u + frac * (v - u)
                at = (turn, f, e, slice(8 * k, 8 * k + 8), slice(None))
                rhs[at] = jnp.where(hit, mixed, rhs[at])

    for side, far_ref in enumerate((far_low_ref, far_high_ref)):
        lift(far_ref, slots)

        def place(n, _, side=side, far_ref=far_ref):
            address = notes_ref[4 + side * -(-slots // LANES) + n // LANES, n % LANES]
            put(side, address >> 3, address & 7, far_ref, n)
            return 0

        lax.fori_loop(0, jnp.minimum(notes_ref[2 + side, LANES - 1], slots), place, 0)

    sub = lax.broadcasted_iota(jnp.int32, (8, LEV), 0)
    bottom, last = sub == 0, sub == 7

    def tile(f, _):
        s = stiff_ref[f]
        prev = 1.0
        for sweep in range(2 * TRAJ):
            omega = OMEGAS[sweep % 2]
            alpha = jnp.broadcast_to((1.0 - omega - 4.0 * omega * s) * (prev / omega), (8, LEV))
            beta = jnp.broadcast_to(s * prev, (8, LEV))
            prev = omega
            turn = sweep // 2
            src, dst = (x_ref, xa, xb, xa)[sweep], (xa, xb, xa, None)[sweep]

            def load(e, src=src):
                return [src[f, e, 8 * k : 8 * k + 8, :] for k in range(groups)]

            def block(group, carry, load=load, dst=dst, alpha=alpha, beta=beta, turn=turn, omega=omega):
                south, mid = carry
                for v in range(SWEEP_ROWS):
                    e = group * SWEEP_ROWS + v
                    north = load(e + 1)
                    left, right = mid[0], mid[groups - 1]
                    first, final = mid[1], mid[groups - 2]
                    from_west = [pltpu.roll(x, 1, 0) for x in (left, final, right)]
                    from_east = [pltpu.roll(x, 7, 0) for x in (left, first, right)]
                    wests = [from_west[0], jnp.where(bottom, from_west[0], from_west[1])]
                    wests += mid[1 : groups - 2] + [jnp.where(bottom, from_west[1], from_west[2])]
                    easts = [jnp.where(last, from_east[1], from_east[0])] + mid[2 : groups - 1]
                    easts += [jnp.where(last, from_east[2], from_east[1]), from_east[2]]
                    for k in range(groups):
                        around = (south[k] + north[k]) + (wests[k] + easts[k])
                        new = alpha * mid[k] + beta * around + rhs[turn, f, e, 8 * k : 8 * k + 8, :]
                        if dst is not None:
                            dst[f, e, 8 * k : 8 * k + 8, :] = new
                        elif k in (0, groups - 1):
                            nat[f, e, 8 * k : 8 * k + 8, :] = new * omega
                        else:
                            nat[f, e, pl.ds(8 + k - 1, 8, stride=groups - 2), :] = new * omega
                    south, mid = mid, north
                return south, mid

            lax.fori_loop(0, rows // SWEEP_ROWS, block, ([zero] * groups, load(0)))

        lanes = pl.ds(pl.multiple_of(f * LEV, LEV), LEV)
        part = nat.at[f, pl.ds(own0, lat_rows), pl.ds(NEAR, cols), :]
        pltpu.make_async_copy(part, out_any.at[:, :, lanes], sems.at[f]).start()
        return 0

    lax.fori_loop(0, tiles, tile, 0)
    for f in range(tiles):
        part = nat.at[f, pl.ds(own0, lat_rows), pl.ds(NEAR, cols), :]
        pltpu.make_async_copy(part, out_any.at[:, :, pl.ds(f * LEV, LEV)], sems.at[f]).wait()
    for keep in keeps:
        keep.wait()


def shards(state, dep_shift, dep_frac, stiff):
    lat_rows, cols, width = state.shape
    tiles = width // LEV
    rows = lat_rows + NEAR
    wide = cols + 2 * NEAR
    band = cols + 2 * SIDE
    kinds = 2 * TRAJ
    lat = lax.axis_index("lat")
    low = lat == 0
    right, left = ring("lon", 1), ring("lon", -1)
    swap = ring("lat", 1)
    info = lat[None]
    shape = functools.partial(jax.ShapeDtypeStruct, dtype=jnp.float32)
    smem = pl.BlockSpec(memory_space=pltpu.SMEM)
    vmem = pl.BlockSpec(memory_space=pltpu.VMEM)
    anywhere = pl.BlockSpec(memory_space=pl.ANY)
    hbm = pl.BlockSpec(memory_space=pltpu.HBM)

    is_shift = jnp.arange(2)[:, None, None, None] == 0
    dep = jnp.where(is_shift, dep_shift[None].astype(jnp.float32), dep_frac[None]).reshape(kinds, lat_rows, cols)
    near = shape((lat_rows * NEAR, width))
    own, edge, near_left, near_right = pl.pallas_call(
        start_kernel,
        out_shape=(shape((kinds, cols, LANES)), shape((NEAR, cols, width)), near, near),
        in_specs=[smem, vmem, hbm],
        out_specs=(vmem,) * 4,
        scratch_shapes=[
            pltpu.VMEM((LANES, LANES), jnp.float32),
            pltpu.VMEM((2, lat_rows, 8, width), jnp.float32),
            pltpu.SemaphoreType.DMA((3,)),
        ],
        compiler_params=pltpu.CompilerParams(vmem_limit_bytes=16 * 2**20),
    )(info, dep, state)
    other = lax.ppermute(own, "lat", swap)
    edge = lax.ppermute(edge, "lat", swap)
    some = lat_rows // 4 * NEAR
    first = shape((8 + some, width))
    second = shape((rows * NEAR - some, width))
    left_a, right_a, left_b, right_b, dep = pl.pallas_call(
        functools.partial(second_kernel, rows=rows),
        out_shape=(first, first, second, second, shape((kinds, cols, LANES))),
        in_specs=[smem] + [vmem] * 5,
        out_specs=(vmem,) * 5,
        compiler_params=pltpu.CompilerParams(vmem_limit_bytes=4 * 2**20),
    )(info, own, other, edge, near_left, near_right)
    low_a = lax.ppermute(right_a, "lon", right)
    high_a = lax.ppermute(left_a, "lon", left)
    low_b = lax.ppermute(right_b, "lon", right)
    high_b = lax.ppermute(left_b, "lon", left)

    few = shape((SLOTS, width))
    size = rows * 8
    send_low, send_high, notes, over, around = pl.pallas_call(
        functools.partial(pack_kernel, rows=rows, slots=SLOTS),
        out_shape=(
            few,
            few,
            jax.ShapeDtypeStruct((8, LANES), jnp.int32),
            jax.ShapeDtypeStruct((1,), jnp.int32),
            shape((kinds, wide, LANES)),
        ),
        in_specs=[smem] + [vmem] * 5,
        out_specs=(vmem, vmem, vmem, smem, vmem),
        scratch_shapes=[pltpu.SMEM((8, LANES), jnp.int32), pltpu.SemaphoreType.DMA(())],
        compiler_params=pltpu.CompilerParams(vmem_limit_bytes=4 * 2**20),
        cost_estimate=pl.CostEstimate(flops=0, bytes_accessed=40 * 2**20, transcendentals=0),
    )(info, dep, state.reshape(lat_rows * cols, width), edge.reshape(NEAR * cols, width), low_a, high_a)
    far_high = lax.ppermute(send_low, "lon", left)
    far_low = lax.ppermute(send_high, "lon", right)

    per_row = shape((rows, TRAJ * wide, LANES))
    def weights(around):
        return pl.pallas_call(
            functools.partial(weights_kernel, rows=rows),
            out_shape=(per_row, per_row, shape((2, TRAJ, rows, 8, LANES)), shape(around.shape)),
            in_specs=[vmem],
            out_specs=(vmem, vmem, vmem, hbm),
            scratch_shapes=[pltpu.SemaphoreType.DMA(())],
            compiler_params=pltpu.CompilerParams(vmem_limit_bytes=8 * 2**20),
        )(around)

    pick, frac, met, around = weights(around)
    low_b, high_b, pick = lax.optimization_barrier((low_b, high_b, pick))

    rhs_shape = shape((TRAJ, tiles, rows, wide, LEV))
    x_shape = (tiles, rows + 1, wide, LEV)

    def gather(state, edge, low_a, high_a, low_b, high_b, pick, frac):
        return pl.pallas_call(
            gather_kernel,
            out_shape=(rhs_shape, shape(x_shape)) + tuple(shape(x.shape) for x in (edge, low_a, high_a, low_b, high_b)),
            in_specs=[smem, hbm, anywhere] + [vmem] * 6,
            out_specs=(vmem, vmem) + (hbm,) * 5,
            scratch_shapes=[
                pltpu.VMEM((tiles, rows, cols + 2 * SIDE, LEV), jnp.float32),
                pltpu.SemaphoreType.DMA((2 * tiles + 5,)),
            ],
            compiler_params=pltpu.CompilerParams(vmem_limit_bytes=12 * 2**20),
            cost_estimate=pl.CostEstimate(flops=0, bytes_accessed=2**20, transcendentals=0),
        )(info, state, edge, low_a, high_a, low_b, high_b, pick, frac)

    def finish(slots, notes, far_low, far_high, met, frac, x, rhs):
        return pl.pallas_call(
            functools.partial(main_kernel, slots=slots),
            out_shape=(shape(state.shape), rhs_shape, shape(far_low.shape), shape(far_high.shape)),
            in_specs=[smem] * 2 + [vmem] * 7,
            out_specs=(hbm, vmem, hbm, hbm),
            scratch_shapes=[
                pltpu.VMEM((slots, width), jnp.float32),
                pltpu.VMEM(x_shape, jnp.float32),
                pltpu.VMEM(x_shape, jnp.float32),
                pltpu.VMEM((tiles, rows, wide, LEV), jnp.float32),
                pltpu.SemaphoreType.DMA((tiles + 2,)),
            ],
            input_output_aliases={8: 1},
            compiler_params=pltpu.CompilerParams(vmem_limit_bytes=16 * 2**20),
        )(info, notes, far_low, far_high, met, frac, stiff.reshape(tiles, 1, LEV), x, rhs)

    rhs, x, *messages = gather(state, edge, low_a, high_a, low_b, high_b, pick, frac)
    out, _, far_low, far_high = finish(SLOTS, notes, far_low, far_high, met, frac, x, rhs)

    def whole():
        counts = notes[:4, LANES - 1]
        most = jnp.maximum(counts[:2], counts[2:])
        over_left, over_right = most[0] > SLOTS, most[1] > SLOTS
        field = jnp.concatenate([state, messages[0]], axis=0)
        at_left = field[:, NEAR : NEAR + 8].reshape(size, width)
        at_right = field[:, cols - NEAR - 8 : cols - NEAR][:, ::-1].reshape(size, width)
        even = lax.axis_index("lon") % 2 == 0
        nothing = jnp.zeros((size, width), jnp.float32)
        got_even = lax.cond(
            jnp.where(even, over_right, over_left),
            lambda: lax.ppermute(jnp.where(even, at_right, at_left), "lon", pairs("lon", 0)),
            lambda: nothing,
        )
        got_odd = lax.cond(
            jnp.where(even, over_left, over_right),
            lambda: lax.ppermute(jnp.where(even, at_left, at_right), "lon", pairs("lon", 1)),
            lambda: nothing,
        )
        lists = -(-size // LANES)
        every = jnp.arange(lists * LANES, dtype=jnp.int32).reshape(lists, LANES)
        more, got = [], []
        for side, (over_side, some) in enumerate(((over_left, far_low), (over_right, far_high))):
            complete = jnp.where((side == 1) == even, got_even, got_odd)
            few = jnp.pad(notes[4 + side : 5 + side], ((0, lists - 1), (0, 0)))
            more.append(jnp.where(over_side, every, few))
            got.append(jnp.where(over_side, complete, jnp.pad(some, ((0, size - SLOTS), (0, 0)))))
        many = jnp.where(jnp.stack([over_left, over_right]), size, counts[2:])
        many = jnp.broadcast_to(jnp.concatenate([counts[:2], many])[:, None], (4, LANES))
        pick, frac, met, _ = weights(around)
        rhs, x, *_ = gather(state, *messages, pick, frac)
        return finish(size, jnp.concatenate([many] + more), got[0], got[1], met, frac, x, rhs)[0]

    return lax.cond(over[0] > 0, whole, lambda: out)


def solution(mesh):
    in_specs = (
        P(("member", "lat"), "lon", None),
        P(None, ("member", "lat"), "lon"),
        P(None, ("member", "lat"), "lon"),
        P(),
    )
    out_specs = P(("member", "lat"), "lon", None)
    return jax.shard_map(shards, mesh=mesh, in_specs=in_specs, out_specs=out_specs, check_vma=False)
```

```python
import functools

import jax
import jax.numpy as jnp
from jax import lax
from jax.experimental import pallas as pl
from jax.experimental.pallas import tpu as pltpu
from jax.sharding import PartitionSpec as P

LEV = 128
TRAJ = 2
REACH = 8
OMEGAS = (0.4227, 0.8104)

NEAR = 2 * TRAJ
FAR = REACH - 1
SLOTS = 80
LANES = 128
SIDE = 8
UP_ROWS = 6
SWEEP_ROWS = 17


def ring(axis, step):
    count = lax.axis_size(axis)
    return [(i, (i + step) % count) for i in range(count)]


def pairs(axis, start):
    count = lax.axis_size(axis)
    edges = [(i, (i + 1) % count) for i in range(start, count, 2)]
    return edges + [(b, a) for a, b in edges]


def turn_kernel(shift_ref, frac_ref, own_ref, pad):
    turns, rows, cols = shift_ref.shape
    pad[...] = jnp.zeros_like(pad)
    for kind in range(2 * turns):
        value = shift_ref[kind].astype(jnp.float32) if kind < turns else frac_ref[kind - turns]
        pad[0:rows, 0:cols] = value
        own_ref[kind] = jnp.transpose(pad[...])[0:cols, :]


def start_kernel(info_ref, state_ref, edge_ref, left_ref, right_ref, sides, sems):
    rows, cols, _ = state_ref.shape
    edge_row = jnp.where(info_ref[0] == 0, rows - NEAR, 0)
    fetch = [
        pltpu.make_async_copy(state_ref.at[:, pl.ds(0, 8), :], sides.at[0], sems.at[0]),
        pltpu.make_async_copy(state_ref.at[:, pl.ds(cols - 8, 8), :], sides.at[1], sems.at[1]),
        pltpu.make_async_copy(state_ref.at[pl.ds(edge_row, NEAR)], edge_ref, sems.at[2]),
    ]
    for copy in fetch:
        copy.start()
    for side, (first, ref) in enumerate(((0, left_ref), (8 - NEAR, right_ref))):
        fetch[side].wait()
        for r in range(0, rows, 2):
            two = jnp.concatenate([sides[side, r + v, first : first + NEAR, :] for v in range(2)], axis=0)
            ref[r * NEAR : (r + 2) * NEAR, :] = two
    fetch[2].wait()


def second_kernel(
    info_ref,
    own_ref,
    next_ref,
    edge_ref,
    left_ref,
    right_ref,
    left_a_ref,
    right_a_ref,
    left_b_ref,
    right_b_ref,
    dep_ref,
    *,
    rows,
):
    kinds, cols, _ = own_ref.shape
    low = info_ref[0] == 0
    lat_rows = rows - NEAR
    lane = lax.broadcasted_iota(jnp.int32, (cols, LANES), 1)
    head = jnp.zeros((8, left_ref.shape[1]), jnp.float32)
    left_a_ref[0:8, :] = head
    right_a_ref[0:8, :] = head
    for kind in range(kinds):
        own, other = own_ref[kind], next_ref[kind]
        other = jnp.where(low, pltpu.roll(other, lat_rows, 1), pltpu.roll(other, NEAR, 1))
        both = jnp.where(lane < lat_rows, own, other)
        dep_ref[kind] = both
        left_a_ref[0:NEAR, kind * LANES : (kind + 1) * LANES] = both[0:NEAR, :]
        right_a_ref[0:NEAR, kind * LANES : (kind + 1) * LANES] = both[cols - NEAR : cols, :]
    some = left_a_ref.shape[0] - 8
    rest = lat_rows * NEAR - some
    left_a_ref[8 : 8 + some, :] = left_ref[0:some, :]
    right_a_ref[8 : 8 + some, :] = right_ref[0:some, :]
    left_b_ref[0:rest, :] = left_ref[some : some + rest, :]
    right_b_ref[0:rest, :] = right_ref[some : some + rest, :]
    for r in range(NEAR):
        at = slice(rest + r * NEAR, rest + (r + 1) * NEAR)
        left_b_ref[at, :] = edge_ref[r, 0:NEAR, :]
        right_b_ref[at, :] = edge_ref[r, cols - NEAR : cols, :]


def pack_kernel(
    info_ref,
    dep_ref,
    state_ref,
    edge_ref,
    from_left_ref,
    from_right_ref,
    low_ref,
    high_ref,
    notes_ref,
    over,
    wide_ref,
    notes,
    sem,
    *,
    rows,
    slots,
):
    kinds, cols, _ = dep_ref.shape
    wide = cols + 2 * NEAR
    lat_rows = rows - NEAR
    low = info_ref[0] == 0
    for kind in range(kinds):
        lanes = slice(kind * LANES, (kind + 1) * LANES)
        wide_ref[kind, 0:NEAR, :] = from_left_ref[0:NEAR, lanes]
        wide_ref[kind, NEAR : NEAR + cols, :] = dep_ref[kind]
        wide_ref[kind, NEAR + cols : wide, :] = from_right_ref[0:NEAR, lanes]

    lane = lax.broadcasted_iota(jnp.int32, (1, LANES), 1)
    beyond = jnp.where(low, lane - lat_rows + 1, rows - lane)
    beyond = jnp.where(lane < lat_rows, 0, jnp.where(lane < rows, beyond, rows))
    reach = [NEAR - 1 - 2 * turn for turn in range(TRAJ)]
    groups = (
        ([0] * TRAJ, 0, 1),
        ([cols + NEAR - r for r in reach], cols - 1, -1),
        ([NEAR - r for r in reach], -1, -1),
        ([cols] * TRAJ, cols, 1),
    )
    totals = []
    for first, anchor, sign in groups:
        total = jnp.zeros((1, LANES), jnp.int32)
        for turn in range(TRAJ):
            for q in range(first[turn], first[turn] + NEAR + reach[turn]):
                target = wide_ref[turn, q : q + 1, :].astype(jnp.int32) + (q - NEAR)
                j = sign * (target - anchor) - NEAR
                hit = (j >= 0) & (j < FAR) & (beyond <= reach[turn])
                total = total | jnp.where(hit, jnp.left_shift(1, jnp.maximum(j, 0)), 0)
        totals.append(total)
    totals = jnp.concatenate(totals + [jnp.zeros((8 - len(groups), LANES), jnp.int32)], axis=0)

    hits = [(totals >> j) & 1 for j in range(FAR)]
    in_row = sum(hits[1:], hits[0])
    upto, lanes8 = in_row, lax.broadcasted_iota(jnp.int32, (8, LANES), 1)
    for d in (1, 2, 4, 8, 16, 32, 64):
        upto = upto + jnp.where(lanes8 >= d, pltpu.roll(upto, d, 1), 0)
    place, places = upto - in_row, []
    for hit in hits:
        places.append(jnp.where(hit == 1, place, -1))
        place = place + hit
    n = lax.broadcasted_iota(jnp.int32, (slots, LANES), 0)
    diagonal = n == lax.broadcasted_iota(jnp.int32, (slots, LANES), 1)
    addresses = (
        (2, 8, 0, 1),
        (3, 8, 0, 1),
        (0, cols, NEAR, 1),
        (1, cols, cols - 1 - NEAR, -1),
    )
    notes_ref[0 : len(groups), :] = upto[0 : len(groups)]
    for i, (which, stride, first, sign) in enumerate(addresses):
        found = jnp.zeros((slots, LANES), jnp.float32)
        for j in range(FAR):
            address = (lane * stride + (first + sign * j)).astype(jnp.float32)
            found = found + jnp.where(places[j][which : which + 1] == n, address, 0.0)
        found = jnp.where(diagonal, jnp.sum(found, axis=1, keepdims=True), 0.0)
        notes_ref[len(groups) + i : len(groups) + i + 1, :] = jnp.sum(found, axis=0, keepdims=True).astype(jnp.int32)
    copy = pltpu.make_async_copy(notes_ref, notes, sem)
    copy.start()
    copy.wait()
    sent = [notes[side, LANES - 1] for side in range(2)]
    most = jnp.maximum(jnp.maximum(sent[0], sent[1]), jnp.maximum(notes[2, LANES - 1], notes[3, LANES - 1]))
    over[0] = (most > slots).astype(jnp.int32)
    own = lat_rows * cols

    def gather(group, _):
        for u in range(8):
            n = group * 8 + u
            for side, ref in enumerate((low_ref, high_ref)):
                address = jnp.minimum(notes[6 + side, n], own - 1)
                ref[pl.ds(n, 1), :] = state_ref[pl.ds(address, 1), :]
        return 0

    lax.fori_loop(0, slots // 8, gather, 0)

    def gather_edge(side, ref):
        def body(n):
            ref[pl.ds(n, 1), :] = edge_ref[pl.ds(notes[6 + side, n] - own, 1), :]
            return n - 1

        start = jnp.minimum(sent[side], slots) - 1
        lax.while_loop(lambda n: (n >= 0) & (notes[6 + side, jnp.maximum(n, 0)] >= own), body, start)

    gather_edge(0, low_ref)
    gather_edge(1, high_ref)


def arranged(ref, index, start, groups):
    middle = groups - 2
    parts = [ref[index + (pl.ds(start, 8), slice(None))]]
    parts += [ref[index + (pl.ds(start + 8 + k, 8, stride=middle), slice(None))] for k in range(middle)]
    return parts + [ref[index + (pl.ds(start + 8 * (groups - 1), 8), slice(None))]]


def weights_kernel(wide_ref, pick_ref, frac_ref, far_ref, kept_ref, sem, *, rows):
    kinds, wide, _ = wide_ref.shape
    cols = wide - 2 * NEAR
    keep = pltpu.make_async_copy(wide_ref, kept_ref, sem)
    keep.start()
    groups, band = wide // 8, cols + 2 * SIDE
    place = lax.broadcasted_iota(jnp.int32, (8, LANES), 1)
    place = jnp.where(place < band, place, place - band)
    place = jnp.where(place < band, place, -LANES).astype(jnp.float32)
    sub = lax.broadcasted_iota(jnp.int32, (8, LANES), 0)
    firsts = [sub] + [8 + k + sub * (groups - 2) for k in range(groups - 2)] + [8 * (groups - 1) + sub]
    parts = []
    for turn in range(TRAJ):
        for k, shift in enumerate(arranged(wide_ref, (turn,), 0, groups)):
            parts.append(shift + (firsts[k] - NEAR).astype(jnp.float32))
    fracs = [frac for turn in range(TRAJ) for frac in arranged(wide_ref, (TRAJ + turn,), 0, groups)]
    highs = [frac.astype(jnp.bfloat16).astype(jnp.float32) for frac in fracs]
    parts += highs + [frac - high for frac, high in zip(fracs, highs)]
    table = jnp.concatenate(parts, axis=0).astype(jnp.bfloat16)
    row = lax.broadcasted_iota(jnp.int32, (LANES, LANES), 0)
    count = TRAJ * wide
    for m in range(rows):
        spread = jnp.dot(table, jnp.where(row == m, 1.0, 0.0).astype(jnp.bfloat16), preferred_element_type=jnp.float32)
        frac_ref[m] = spread[count : 2 * count] + spread[2 * count :]
        for n in range(TRAJ * groups):
            column = spread[8 * n : 8 * n + 8]
            pick_ref[m, 8 * n : 8 * n + 8, :] = jnp.where(column + SIDE == place, 1.0, 0.0)
            turn, k = divmod(n, groups)
            if k == 0:
                far_ref[0, turn, m] = -1 - NEAR - column
            if k == groups - 1:
                far_ref[1, turn, m] = column - (cols + NEAR)
    keep.wait()


def gather_kernel(
    info_ref,
    state_ref,
    edge_ref,
    low_a_ref,
    high_a_ref,
    low_b_ref,
    high_b_ref,
    pick_ref,
    frac_ref,
    rhs,
    x_ref,
    *rest,
):
    *kept, ext, sems = rest
    lat_rows, cols, width = state_ref.shape
    tiles = width // LEV
    rows = lat_rows + NEAR
    wide = cols + 2 * NEAR
    groups, band = wide // 8, cols + 2 * SIDE
    own0 = jnp.where(info_ref[0] == 0, 0, NEAR)
    ext0 = jnp.where(info_ref[0] == 0, lat_rows, 0)
    copies = []
    for f in range(tiles):
        lanes = pl.ds(f * LEV, LEV)
        for i, (ref, first, count) in enumerate(((state_ref, own0, lat_rows), (edge_ref, ext0, NEAR))):
            copies.append(
                pltpu.make_async_copy(
                    ref.at[:, :, lanes],
                    ext.at[f, pl.ds(first, count), pl.ds(SIDE, cols), :],
                    sems.at[2 * f + i],
                )
            )
            copies[-1].start()
    keeps = []
    for i, (source, target) in enumerate(zip((edge_ref, low_a_ref, high_a_ref, low_b_ref, high_b_ref), kept)):
        keeps.append(pltpu.make_async_copy(source, target, sems.at[2 * tiles + i]))
        keeps[-1].start()
    zero = jnp.zeros((8, LEV), jnp.float32)
    for f in range(tiles):
        for k in range(groups):
            x_ref[f, rows, 8 * k : 8 * k + 8, :] = zero

    first = (low_a_ref.shape[0] - 8) // NEAR
    blank = jnp.zeros((SIDE - NEAR, LEV), jnp.float32)

    def near(m, start, low, high):
        e = jnp.where(m < lat_rows, own0 + m, ext0 + m - lat_rows)
        at = pl.ds(pl.multiple_of(start, 8), 2 * NEAR)
        west, east = low[at, :], high[at, :]
        for f in range(tiles):
            for v in range(2):
                part = (slice(v * NEAR, (v + 1) * NEAR), slice(f * LEV, (f + 1) * LEV))
                ext[f, e + v, 0:SIDE, :] = jnp.concatenate([blank, west[part]], axis=0)
                ext[f, e + v, SIDE + cols : band, :] = jnp.concatenate([east[part], blank], axis=0)

    def near_a(n, _):
        near(2 * n, 8 + 2 * NEAR * n, low_a_ref, high_a_ref)
        return 0

    def near_b(n, _):
        near(first + 2 * n, 2 * NEAR * n, low_b_ref, high_b_ref)
        return 0

    lax.fori_loop(0, first // 2, near_a, 0)
    lax.fori_loop(0, (rows - first) // 2, near_b, 0)
    for copy in copies:
        copy.wait()

    top = lax.broadcasted_iota(jnp.int32, (wide, LEV), 1) == LEV - 1

    def upstream(group, _):
        for v in range(UP_ROWS):
            e = group * UP_ROWS + v
            own = (e >= own0) & (e < own0 + lat_rows)
            m = jnp.where(own, e - own0, e - ext0 + lat_rows)
            his, los = [], []
            for f in range(tiles):
                value = ext[f, e]
                hi = value.astype(jnp.bfloat16)
                his.append(hi)
                los.append((value - hi.astype(jnp.float32)).astype(jnp.bfloat16))
                for k, part in enumerate(arranged(ext, (f, e), SIDE - NEAR, groups)):
                    x_ref[f, e, 8 * k : 8 * k + 8, :] = part
            field = jnp.concatenate([jnp.concatenate(his, axis=1), jnp.concatenate(los, axis=1)], axis=0)
            pick = pick_ref[m].astype(jnp.bfloat16)[:, : 2 * band]
            got = jnp.dot(pick, field, preferred_element_type=jnp.float32)
            for turn in range(TRAJ):
                frac = frac_ref[m, turn * wide : (turn + 1) * wide, :]
                for f in range(tiles):
                    u = got[turn * wide : (turn + 1) * wide, f * LEV : (f + 1) * LEV]
                    up = jnp.where(top, u, pltpu.roll(u, LEV - 1, 1))
                    rhs[turn, f, e] = u + frac * (up - u)
        return 0

    lax.fori_loop(0, rows // UP_ROWS, upstream, 0)
    for keep in keeps:
        keep.wait()


def main_kernel(
    info_ref,
    notes_ref,
    far_low_ref,
    far_high_ref,
    met_ref,
    frac_ref,
    stiff_ref,
    x_ref,
    rhs_in,
    out_any,
    rhs,
    low_kept,
    high_kept,
    ups,
    xa,
    xb,
    nat,
    sems,
    *,
    slots,
):
    lat_rows, cols, width = out_any.shape
    tiles = width // LEV
    rows = lat_rows + NEAR
    wide = cols + 2 * NEAR
    groups = wide // 8
    own0 = jnp.where(info_ref[0] == 0, 0, NEAR)
    ext0 = jnp.where(info_ref[0] == 0, lat_rows, 0)
    keeps = [
        pltpu.make_async_copy(far_low_ref, low_kept, sems.at[tiles]),
        pltpu.make_async_copy(far_high_ref, high_kept, sems.at[tiles + 1]),
    ]
    for keep in keeps:
        keep.start()
    zero = jnp.zeros((8, LEV), jnp.float32)
    for f in range(tiles):
        for k in range(groups):
            xa[f, rows, 8 * k : 8 * k + 8, :] = zero
            xb[f, rows, 8 * k : 8 * k + 8, :] = zero

    def lift(source, ups, count):
        def block(n, _):
            at = pl.ds(pl.multiple_of(n * 8, 8), 8)
            lane = lax.broadcasted_iota(jnp.int32, (8, LEV), 1)
            for f in range(tiles):
                lanes = slice(f * LEV, (f + 1) * LEV)
                u = source[at, lanes]
                ups[at, lanes] = jnp.where(lane == LEV - 1, u, pltpu.roll(u, LEV - 1, 1))
            return 0

        lax.fori_loop(0, count // 8, block, 0)

    def put(side, m, j, n):
        k = 0 if side == 0 else groups - 1
        e = jnp.where(m < lat_rows, own0 + m, ext0 + m - lat_rows)
        column, up = (far_low_ref, far_high_ref)[side][pl.ds(n, 1), :], ups[side, pl.ds(n, 1), :]
        for turn in range(TRAJ):
            hit = met_ref[side, turn, m] == j.astype(jnp.float32)
            frac = frac_ref[m, turn * wide + 8 * k : turn * wide + 8 * k + 8, :]
            for f in range(tiles):
                u, v = column[:, f * LEV : (f + 1) * LEV], up[:, f * LEV : (f + 1) * LEV]
                mixed = u + frac * (v - u)
                at = (turn, f, e, slice(8 * k, 8 * k + 8), slice(None))
                rhs[at] = jnp.where(hit, mixed, rhs[at])

    fars = (far_low_ref, far_high_ref)
    counts = [jnp.minimum(notes_ref[2 + side, LANES - 1], slots) for side in range(2)]
    for side in range(2):
        lift(fars[side], ups.at[side], slots)

    def place(n, _):
        for side in range(2):
            address = notes_ref[4 + side * -(-slots // LANES) + n // LANES, n % LANES]
            put(side, address >> 3, jnp.where(n < counts[side], address & 7, -LANES), n)
        return 0

    lax.fori_loop(0, jnp.maximum(counts[0], counts[1]), place, 0)

    sub = lax.broadcasted_iota(jnp.int32, (8, LEV), 0)
    bottom, last = sub == 0, sub == 7

    def tile(f, _):
        s = stiff_ref[f]
        prev = 1.0
        for sweep in range(2 * TRAJ):
            omega = OMEGAS[sweep % 2]
            alpha = jnp.broadcast_to((1.0 - omega - 4.0 * omega * s) * (prev / omega), (8, LEV))
            beta = jnp.broadcast_to(s * prev, (8, LEV))
            prev = omega
            turn = sweep // 2
            src, dst = (x_ref, xa, xb, xa)[sweep], (xa, xb, xa, None)[sweep]
            beyond = 2 * TRAJ - 1 - sweep
            start = jnp.maximum(own0 - beyond, 0)
            step = max(d for d in range(1, SWEEP_ROWS + 1) if (lat_rows + beyond) % d == 0)

            def load(e, src=src):
                return [src[f, e, 8 * k : 8 * k + 8, :] for k in range(groups)]

            def block(
                group, carry, load=load, dst=dst, alpha=alpha, beta=beta, turn=turn, omega=omega, start=start, step=step
            ):
                south, mid = carry
                for v in range(step):
                    e = start + group * step + v
                    north = load(e + 1)
                    left, right = mid[0], mid[groups - 1]
                    first, final = mid[1], mid[groups - 2]
                    from_west = [pltpu.roll(x, 1, 0) for x in (left, final, right)]
                    from_east = [pltpu.roll(x, 7, 0) for x in (left, first, right)]
                    wests = [from_west[0], jnp.where(bottom, from_west[0], from_west[1])]
                    wests += mid[1 : groups - 2] + [jnp.where(bottom, from_west[1], from_west[2])]
                    easts = [jnp.where(last, from_east[1], from_east[0])] + mid[2 : groups - 1]
                    easts += [jnp.where(last, from_east[2], from_east[1]), from_east[2]]
                    for k in range(groups):
                        around = (south[k] + north[k]) + (wests[k] + easts[k])
                        new = alpha * mid[k] + beta * around + rhs[turn, f, e, 8 * k : 8 * k + 8, :]
                        if dst is not None:
                            dst[f, e, 8 * k : 8 * k + 8, :] = new
                        elif k in (0, groups - 1):
                            nat[f, e, 8 * k : 8 * k + 8, :] = new * omega
                        else:
                            nat[f, e, pl.ds(8 + k - 1, 8, stride=groups - 2), :] = new * omega
                    south, mid = mid, north
                return south, mid

            before = [jnp.where(start == 0, 0.0, v) for v in load(jnp.maximum(start - 1, 0))]
            lax.fori_loop(0, (lat_rows + beyond) // step, block, (before, load(start)))

        lanes = pl.ds(pl.multiple_of(f * LEV, LEV), LEV)
        part = nat.at[f, pl.ds(own0, lat_rows), pl.ds(NEAR, cols), :]
        pltpu.make_async_copy(part, out_any.at[:, :, lanes], sems.at[f]).start()
        return 0

    lax.fori_loop(0, tiles, tile, 0)
    for f in range(tiles):
        part = nat.at[f, pl.ds(own0, lat_rows), pl.ds(NEAR, cols), :]
        pltpu.make_async_copy(part, out_any.at[:, :, pl.ds(f * LEV, LEV)], sems.at[f]).wait()
    for keep in keeps:
        keep.wait()


def shards(state, dep_shift, dep_frac, stiff):
    lat_rows, cols, width = state.shape
    tiles = width // LEV
    rows = lat_rows + NEAR
    wide = cols + 2 * NEAR
    band = cols + 2 * SIDE
    kinds = 2 * TRAJ
    lat = lax.axis_index("lat")
    low = lat == 0
    right, left = ring("lon", 1), ring("lon", -1)
    swap = ring("lat", 1)
    info = lat[None]
    shape = functools.partial(jax.ShapeDtypeStruct, dtype=jnp.float32)
    smem = pl.BlockSpec(memory_space=pltpu.SMEM)
    vmem = pl.BlockSpec(memory_space=pltpu.VMEM)
    anywhere = pl.BlockSpec(memory_space=pl.ANY)
    hbm = pl.BlockSpec(memory_space=pltpu.HBM)

    near = shape((lat_rows * NEAR, width))
    edge, near_left, near_right = pl.pallas_call(
        start_kernel,
        out_shape=(shape((NEAR, cols, width)), near, near),
        in_specs=[smem, hbm],
        out_specs=(vmem,) * 3,
        scratch_shapes=[
            pltpu.VMEM((2, lat_rows, 8, width), jnp.float32),
            pltpu.SemaphoreType.DMA((3,)),
        ],
        compiler_params=pltpu.CompilerParams(vmem_limit_bytes=16 * 2**20),
    )(info, state)
    own = pl.pallas_call(
        turn_kernel,
        out_shape=shape((kinds, cols, LANES)),
        in_specs=[vmem] * 2,
        out_specs=vmem,
        scratch_shapes=[pltpu.VMEM((LANES, LANES), jnp.float32)],
        compiler_params=pltpu.CompilerParams(vmem_limit_bytes=4 * 2**20),
    )(dep_shift, dep_frac)
    other = lax.ppermute(own, "lat", swap)
    edge = lax.ppermute(edge, "lat", swap)
    some = lat_rows // 4 * NEAR
    first = shape((8 + some, width))
    second = shape((rows * NEAR - some, width))
    left_a, right_a, left_b, right_b, dep = pl.pallas_call(
        functools.partial(second_kernel, rows=rows),
        out_shape=(first, first, second, second, shape((kinds, cols, LANES))),
        in_specs=[smem] + [vmem] * 5,
        out_specs=(vmem,) * 5,
        compiler_params=pltpu.CompilerParams(vmem_limit_bytes=4 * 2**20),
    )(info, own, other, edge, near_left, near_right)
    low_a = lax.ppermute(right_a, "lon", right)
    high_a = lax.ppermute(left_a, "lon", left)
    low_b = lax.ppermute(right_b, "lon", right)
    high_b = lax.ppermute(left_b, "lon", left)

    few = shape((SLOTS, width))
    size = rows * 8
    send_low, send_high, notes, over, around = pl.pallas_call(
        functools.partial(pack_kernel, rows=rows, slots=SLOTS),
        out_shape=(
            few,
            few,
            jax.ShapeDtypeStruct((8, LANES), jnp.int32),
            jax.ShapeDtypeStruct((1,), jnp.int32),
            shape((kinds, wide, LANES)),
        ),
        in_specs=[smem] + [vmem] * 5,
        out_specs=(vmem, vmem, vmem, smem, vmem),
        scratch_shapes=[pltpu.SMEM((8, LANES), jnp.int32), pltpu.SemaphoreType.DMA(())],
        compiler_params=pltpu.CompilerParams(vmem_limit_bytes=4 * 2**20),
        cost_estimate=pl.CostEstimate(flops=0, bytes_accessed=40 * 2**20, transcendentals=0),
    )(info, dep, state.reshape(lat_rows * cols, width), edge.reshape(NEAR * cols, width), low_a, high_a)
    far_high = lax.ppermute(send_low, "lon", left)
    far_low = lax.ppermute(send_high, "lon", right)

    per_row = shape((rows, TRAJ * wide, LANES))
    def weights(around):
        return pl.pallas_call(
            functools.partial(weights_kernel, rows=rows),
            out_shape=(per_row, per_row, shape((2, TRAJ, rows, 8, LANES)), shape(around.shape)),
            in_specs=[vmem],
            out_specs=(vmem, vmem, vmem, hbm),
            scratch_shapes=[pltpu.SemaphoreType.DMA(())],
            compiler_params=pltpu.CompilerParams(vmem_limit_bytes=8 * 2**20),
        )(around)

    pick, frac, met, around = weights(around)
    low_b, high_b, pick = lax.optimization_barrier((low_b, high_b, pick))

    rhs_shape = shape((TRAJ, tiles, rows, wide, LEV))
    x_shape = (tiles, rows + 1, wide, LEV)

    def gather(state, edge, low_a, high_a, low_b, high_b, pick, frac):
        return pl.pallas_call(
            gather_kernel,
            out_shape=(rhs_shape, shape(x_shape)) + tuple(shape(x.shape) for x in (edge, low_a, high_a, low_b, high_b)),
            in_specs=[smem, hbm, anywhere] + [vmem] * 6,
            out_specs=(vmem, vmem) + (hbm,) * 5,
            scratch_shapes=[
                pltpu.VMEM((tiles, rows, cols + 2 * SIDE, LEV), jnp.float32),
                pltpu.SemaphoreType.DMA((2 * tiles + 5,)),
            ],
            compiler_params=pltpu.CompilerParams(vmem_limit_bytes=12 * 2**20),
            cost_estimate=pl.CostEstimate(flops=0, bytes_accessed=2**20, transcendentals=0),
        )(info, state, edge, low_a, high_a, low_b, high_b, pick, frac)

    def finish(slots, notes, far_low, far_high, met, frac, x, rhs):
        return pl.pallas_call(
            functools.partial(main_kernel, slots=slots),
            out_shape=(shape(state.shape), rhs_shape, shape(far_low.shape), shape(far_high.shape)),
            in_specs=[smem] * 2 + [vmem] * 7,
            out_specs=(hbm, vmem, hbm, hbm),
            scratch_shapes=[
                pltpu.VMEM((2, slots, width), jnp.float32),
                pltpu.VMEM(x_shape, jnp.float32),
                pltpu.VMEM(x_shape, jnp.float32),
                pltpu.VMEM((tiles, rows, wide, LEV), jnp.float32),
                pltpu.SemaphoreType.DMA((tiles + 2,)),
            ],
            input_output_aliases={8: 1},
            compiler_params=pltpu.CompilerParams(vmem_limit_bytes=16 * 2**20),
        )(info, notes, far_low, far_high, met, frac, stiff.reshape(tiles, 1, LEV), x, rhs)

    rhs, x, *messages = gather(state, edge, low_a, high_a, low_b, high_b, pick, frac)
    out, _, far_low, far_high = finish(SLOTS, notes, far_low, far_high, met, frac, x, rhs)

    def whole():
        counts = notes[:4, LANES - 1]
        most = jnp.maximum(counts[:2], counts[2:])
        over_left, over_right = most[0] > SLOTS, most[1] > SLOTS
        field = jnp.concatenate([state, messages[0]], axis=0)
        at_left = field[:, NEAR : NEAR + 8].reshape(size, width)
        at_right = field[:, cols - NEAR - 8 : cols - NEAR][:, ::-1].reshape(size, width)
        even = lax.axis_index("lon") % 2 == 0
        nothing = jnp.zeros((size, width), jnp.float32)
        got_even = lax.cond(
            jnp.where(even, over_right, over_left),
            lambda: lax.ppermute(jnp.where(even, at_right, at_left), "lon", pairs("lon", 0)),
            lambda: nothing,
        )
        got_odd = lax.cond(
            jnp.where(even, over_left, over_right),
            lambda: lax.ppermute(jnp.where(even, at_left, at_right), "lon", pairs("lon", 1)),
            lambda: nothing,
        )
        lists = -(-size // LANES)
        every = jnp.arange(lists * LANES, dtype=jnp.int32).reshape(lists, LANES)
        more, got = [], []
        for side, (over_side, some) in enumerate(((over_left, far_low), (over_right, far_high))):
            complete = jnp.where((side == 1) == even, got_even, got_odd)
            few = jnp.pad(notes[4 + side : 5 + side], ((0, lists - 1), (0, 0)))
            more.append(jnp.where(over_side, every, few))
            got.append(jnp.where(over_side, complete, jnp.pad(some, ((0, size - SLOTS), (0, 0)))))
        many = jnp.where(jnp.stack([over_left, over_right]), size, counts[2:])
        many = jnp.broadcast_to(jnp.concatenate([counts[:2], many])[:, None], (4, LANES))
        pick, frac, met, _ = weights(around)
        rhs, x, *_ = gather(state, *messages, pick, frac)
        return finish(size, jnp.concatenate([many] + more), got[0], got[1], met, frac, x, rhs)[0]

    return lax.cond(over[0] > 0, whole, lambda: out)


def solution(mesh):
    in_specs = (
        P(("member", "lat"), "lon", None),
        P(None, ("member", "lat"), "lon"),
        P(None, ("member", "lat"), "lon"),
        P(),
    )
    out_specs = P(("member", "lat"), "lon", None)
    return jax.shard_map(shards, mesh=mesh, in_specs=in_specs, out_specs=out_specs, check_vma=False)
```

```python
import functools

import jax
import jax.numpy as jnp
from jax import lax
from jax.experimental import pallas as pl
from jax.experimental.pallas import tpu as pltpu
from jax.sharding import PartitionSpec as P

LEV = 128
TRAJ = 2
REACH = 8
OMEGAS = (0.4227, 0.8104)

NEAR = 2 * TRAJ
FAR = REACH - 1
SLOTS = 80
LANES = 128
SIDE = 8
UP_ROWS = 12
SWEEP_ROWS = 36


def ring(axis, step):
    count = lax.axis_size(axis)
    return [(i, (i + step) % count) for i in range(count)]


def pairs(axis, start):
    count = lax.axis_size(axis)
    edges = [(i, (i + 1) % count) for i in range(start, count, 2)]
    return edges + [(b, a) for a, b in edges]


def turn_kernel(shift_ref, frac_ref, own_ref, pad):
    turns, rows, cols = shift_ref.shape
    pad[...] = jnp.zeros_like(pad)
    for kind in range(2 * turns):
        value = shift_ref[kind].astype(jnp.float32) if kind < turns else frac_ref[kind - turns]
        pad[0:rows, 0:cols] = value
        own_ref[kind] = jnp.transpose(pad[...])[0:cols, :]


def start_kernel(info_ref, state_ref, edge_ref, left_ref, right_ref, sides, sems):
    rows, cols, _ = state_ref.shape
    edge_row = jnp.where(info_ref[0] == 0, rows - NEAR, 0)
    fetch = [
        pltpu.make_async_copy(state_ref.at[:, pl.ds(0, 8), :], sides.at[0], sems.at[0]),
        pltpu.make_async_copy(state_ref.at[:, pl.ds(cols - 8, 8), :], sides.at[1], sems.at[1]),
        pltpu.make_async_copy(state_ref.at[pl.ds(edge_row, NEAR)], edge_ref, sems.at[2]),
    ]
    for copy in fetch:
        copy.start()
    for side, (first, ref) in enumerate(((0, left_ref), (8 - NEAR, right_ref))):
        fetch[side].wait()
        for r in range(0, rows, 2):
            two = jnp.concatenate([sides[side, r + v, first : first + NEAR, :] for v in range(2)], axis=0)
            ref[r * NEAR : (r + 2) * NEAR, :] = two
    fetch[2].wait()


def second_kernel(
    info_ref,
    own_ref,
    next_ref,
    edge_ref,
    left_ref,
    right_ref,
    left_a_ref,
    right_a_ref,
    left_b_ref,
    right_b_ref,
    dep_ref,
    *,
    rows,
):
    kinds, cols, _ = own_ref.shape
    low = info_ref[0] == 0
    lat_rows = rows - NEAR
    lane = lax.broadcasted_iota(jnp.int32, (cols, LANES), 1)
    head = jnp.zeros((8, left_ref.shape[1]), jnp.float32)
    left_a_ref[0:8, :] = head
    right_a_ref[0:8, :] = head
    for kind in range(kinds):
        own, other = own_ref[kind], next_ref[kind]
        other = jnp.where(low, pltpu.roll(other, lat_rows, 1), pltpu.roll(other, NEAR, 1))
        both = jnp.where(lane < lat_rows, own, other)
        dep_ref[kind] = both
        left_a_ref[0:NEAR, kind * LANES : (kind + 1) * LANES] = both[0:NEAR, :]
        right_a_ref[0:NEAR, kind * LANES : (kind + 1) * LANES] = both[cols - NEAR : cols, :]
    some = left_a_ref.shape[0] - 8
    rest = lat_rows * NEAR - some
    left_a_ref[8 : 8 + some, :] = left_ref[0:some, :]
    right_a_ref[8 : 8 + some, :] = right_ref[0:some, :]
    left_b_ref[0:rest, :] = left_ref[some : some + rest, :]
    right_b_ref[0:rest, :] = right_ref[some : some + rest, :]
    for r in range(NEAR):
        at = slice(rest + r * NEAR, rest + (r + 1) * NEAR)
        left_b_ref[at, :] = edge_ref[r, 0:NEAR, :]
        right_b_ref[at, :] = edge_ref[r, cols - NEAR : cols, :]


def pack_kernel(
    info_ref,
    dep_ref,
    state_ref,
    edge_ref,
    from_left_ref,
    from_right_ref,
    low_ref,
    high_ref,
    notes_ref,
    over,
    wide_ref,
    notes,
    sem,
    *,
    rows,
    slots,
):
    kinds, cols, _ = dep_ref.shape
    wide = cols + 2 * NEAR
    lat_rows = rows - NEAR
    low = info_ref[0] == 0
    for kind in range(kinds):
        lanes = slice(kind * LANES, (kind + 1) * LANES)
        wide_ref[kind, 0:NEAR, :] = from_left_ref[0:NEAR, lanes]
        wide_ref[kind, NEAR : NEAR + cols, :] = dep_ref[kind]
        wide_ref[kind, NEAR + cols : wide, :] = from_right_ref[0:NEAR, lanes]

    lane = lax.broadcasted_iota(jnp.int32, (1, LANES), 1)
    beyond = jnp.where(low, lane - lat_rows + 1, rows - lane)
    beyond = jnp.where(lane < lat_rows, 0, jnp.where(lane < rows, beyond, rows))
    reach = [NEAR - 1 - 2 * turn for turn in range(TRAJ)]
    groups = (
        ([0] * TRAJ, 0, 1),
        ([cols + NEAR - r for r in reach], cols - 1, -1),
        ([NEAR - r for r in reach], -1, -1),
        ([cols] * TRAJ, cols, 1),
    )
    totals = []
    for first, anchor, sign in groups:
        total = jnp.zeros((1, LANES), jnp.int32)
        for turn in range(TRAJ):
            for q in range(first[turn], first[turn] + NEAR + reach[turn]):
                target = wide_ref[turn, q : q + 1, :].astype(jnp.int32) + (q - NEAR)
                j = sign * (target - anchor) - NEAR
                hit = (j >= 0) & (j < FAR) & (beyond <= reach[turn])
                total = total | jnp.where(hit, jnp.left_shift(1, jnp.maximum(j, 0)), 0)
        totals.append(total)
    totals = jnp.concatenate(totals + [jnp.zeros((8 - len(groups), LANES), jnp.int32)], axis=0)

    hits = [(totals >> j) & 1 for j in range(FAR)]
    in_row = sum(hits[1:], hits[0])
    upto, lanes8 = in_row, lax.broadcasted_iota(jnp.int32, (8, LANES), 1)
    for d in (1, 2, 4, 8, 16, 32, 64):
        upto = upto + jnp.where(lanes8 >= d, pltpu.roll(upto, d, 1), 0)
    place, places = upto - in_row, []
    for hit in hits:
        places.append(jnp.where(hit == 1, place, -1))
        place = place + hit
    n = lax.broadcasted_iota(jnp.int32, (slots, LANES), 0)
    diagonal = n == lax.broadcasted_iota(jnp.int32, (slots, LANES), 1)
    addresses = (
        (2, 8, 0, 1),
        (3, 8, 0, 1),
        (0, cols, NEAR, 1),
        (1, cols, cols - 1 - NEAR, -1),
    )
    notes_ref[0 : len(groups), :] = upto[0 : len(groups)]
    for i, (which, stride, first, sign) in enumerate(addresses):
        found = jnp.zeros((slots, LANES), jnp.float32)
        for j in range(FAR):
            address = (lane * stride + (first + sign * j)).astype(jnp.float32)
            found = found + jnp.where(places[j][which : which + 1] == n, address, 0.0)
        found = jnp.where(diagonal, jnp.sum(found, axis=1, keepdims=True), 0.0)
        notes_ref[len(groups) + i : len(groups) + i + 1, :] = jnp.sum(found, axis=0, keepdims=True).astype(jnp.int32)
    copy = pltpu.make_async_copy(notes_ref, notes, sem)
    copy.start()
    copy.wait()
    sent = [notes[side, LANES - 1] for side in range(2)]
    most = jnp.maximum(jnp.maximum(sent[0], sent[1]), jnp.maximum(notes[2, LANES - 1], notes[3, LANES - 1]))
    over[0] = (most > slots).astype(jnp.int32)
    own = lat_rows * cols

    def gather(group, _):
        for u in range(8):
            n = group * 8 + u
            for side, ref in enumerate((low_ref, high_ref)):
                address = jnp.minimum(notes[6 + side, n], own - 1)
                ref[pl.ds(n, 1), :] = state_ref[pl.ds(address, 1), :]
        return 0

    lax.fori_loop(0, slots // 8, gather, 0)

    def gather_edge(side, ref):
        def body(n):
            ref[pl.ds(n, 1), :] = edge_ref[pl.ds(notes[6 + side, n] - own, 1), :]
            return n - 1

        start = jnp.minimum(sent[side], slots) - 1
        lax.while_loop(lambda n: (n >= 0) & (notes[6 + side, jnp.maximum(n, 0)] >= own), body, start)

    gather_edge(0, low_ref)
    gather_edge(1, high_ref)


def arranged(ref, index, start, groups):
    middle = groups - 2
    parts = [ref[index + (pl.ds(start, 8), slice(None))]]
    parts += [ref[index + (pl.ds(start + 8 + k, 8, stride=middle), slice(None))] for k in range(middle)]
    return parts + [ref[index + (pl.ds(start + 8 * (groups - 1), 8), slice(None))]]


def weights_kernel(wide_ref, pick_ref, frac_ref, far_ref, kept_ref, sem, *, rows):
    kinds, wide, _ = wide_ref.shape
    cols = wide - 2 * NEAR
    keep = pltpu.make_async_copy(wide_ref, kept_ref, sem)
    keep.start()
    groups, band = wide // 8, cols + 2 * SIDE
    place = lax.broadcasted_iota(jnp.int32, (8, LANES), 1)
    place = jnp.where(place < band, place, place - band)
    place = jnp.where(place < band, place, -LANES).astype(jnp.float32)
    sub = lax.broadcasted_iota(jnp.int32, (8, LANES), 0)
    firsts = [sub] + [8 + k + sub * (groups - 2) for k in range(groups - 2)] + [8 * (groups - 1) + sub]
    parts = []
    for turn in range(TRAJ):
        for k, shift in enumerate(arranged(wide_ref, (turn,), 0, groups)):
            parts.append(shift + (firsts[k] - NEAR).astype(jnp.float32))
    fracs = [frac for turn in range(TRAJ) for frac in arranged(wide_ref, (TRAJ + turn,), 0, groups)]
    highs = [frac.astype(jnp.bfloat16).astype(jnp.float32) for frac in fracs]
    parts += highs + [frac - high for frac, high in zip(fracs, highs)]
    table = jnp.concatenate(parts, axis=0).astype(jnp.bfloat16)
    row = lax.broadcasted_iota(jnp.int32, (LANES, LANES), 0)
    count = TRAJ * wide
    for m in range(rows):
        spread = jnp.dot(table, jnp.where(row == m, 1.0, 0.0).astype(jnp.bfloat16), preferred_element_type=jnp.float32)
        frac_ref[m] = spread[count : 2 * count] + spread[2 * count :]
        for n in range(TRAJ * groups):
            column = spread[8 * n : 8 * n + 8]
            pick_ref[m, 8 * n : 8 * n + 8, :] = jnp.where(column + SIDE == place, 1.0, 0.0)
            turn, k = divmod(n, groups)
            if k == 0:
                far_ref[0, turn, m] = -1 - NEAR - column
            if k == groups - 1:
                far_ref[1, turn, m] = column - (cols + NEAR)
    keep.wait()


def gather_kernel(
    info_ref,
    state_ref,
    edge_ref,
    low_a_ref,
    high_a_ref,
    low_b_ref,
    high_b_ref,
    pick_ref,
    frac_ref,
    rhs,
    x_ref,
    *rest,
):
    *kept, ext, sems = rest
    lat_rows, cols, width = state_ref.shape
    tiles = width // LEV
    rows = lat_rows + NEAR
    wide = cols + 2 * NEAR
    groups, band = wide // 8, cols + 2 * SIDE
    own0 = jnp.where(info_ref[0] == 0, 0, NEAR)
    ext0 = jnp.where(info_ref[0] == 0, lat_rows, 0)
    copies = []
    for f in range(tiles):
        lanes = pl.ds(f * LEV, LEV)
        for i, (ref, first, count) in enumerate(((state_ref, own0, lat_rows), (edge_ref, ext0, NEAR))):
            copies.append(
                pltpu.make_async_copy(
                    ref.at[:, :, lanes],
                    ext.at[f, pl.ds(first, count), pl.ds(SIDE, cols), :],
                    sems.at[2 * f + i],
                )
            )
            copies[-1].start()
    keeps = []
    for i, (source, target) in enumerate(zip((edge_ref, low_a_ref, high_a_ref, low_b_ref, high_b_ref), kept)):
        keeps.append(pltpu.make_async_copy(source, target, sems.at[2 * tiles + i]))
        keeps[-1].start()
    zero = jnp.zeros((8, LEV), jnp.float32)
    for f in range(tiles):
        for k in range(groups):
            x_ref[f, rows, 8 * k : 8 * k + 8, :] = zero

    first = (low_a_ref.shape[0] - 8) // NEAR
    blank = jnp.zeros((SIDE - NEAR, LEV), jnp.float32)

    def near(m, start, low, high):
        e = jnp.where(m < lat_rows, own0 + m, ext0 + m - lat_rows)
        at = pl.ds(pl.multiple_of(start, 8), 2 * NEAR)
        west, east = low[at, :], high[at, :]
        for f in range(tiles):
            for v in range(2):
                part = (slice(v * NEAR, (v + 1) * NEAR), slice(f * LEV, (f + 1) * LEV))
                ext[f, e + v, 0:SIDE, :] = jnp.concatenate([blank, west[part]], axis=0)
                ext[f, e + v, SIDE + cols : band, :] = jnp.concatenate([east[part], blank], axis=0)

    def near_a(n, _):
        near(2 * n, 8 + 2 * NEAR * n, low_a_ref, high_a_ref)
        return 0

    def near_b(n, _):
        near(first + 2 * n, 2 * NEAR * n, low_b_ref, high_b_ref)
        return 0

    lax.fori_loop(0, first // 2, near_a, 0)
    lax.fori_loop(0, (rows - first) // 2, near_b, 0)
    for copy in copies:
        copy.wait()

    top = lax.broadcasted_iota(jnp.int32, (wide, LEV), 1) == LEV - 1

    def upstream(group, _):
        for v in range(UP_ROWS):
            e = group * UP_ROWS + v
            own = (e >= own0) & (e < own0 + lat_rows)
            m = jnp.where(own, e - own0, e - ext0 + lat_rows)
            his, los = [], []
            for f in range(tiles):
                value = ext[f, e]
                hi = value.astype(jnp.bfloat16)
                his.append(hi)
                los.append((value - hi.astype(jnp.float32)).astype(jnp.bfloat16))
                for k, part in enumerate(arranged(ext, (f, e), SIDE - NEAR, groups)):
                    x_ref[f, e, 8 * k : 8 * k + 8, :] = part
            field = jnp.concatenate([jnp.concatenate(his, axis=1), jnp.concatenate(los, axis=1)], axis=0)
            pick = pick_ref[m].astype(jnp.bfloat16)[:, : 2 * band]
            got = jnp.dot(pick, field, preferred_element_type=jnp.float32)
            for turn in range(TRAJ):
                frac = frac_ref[m, turn * wide : (turn + 1) * wide, :]
                for f in range(tiles):
                    u = got[turn * wide : (turn + 1) * wide, f * LEV : (f + 1) * LEV]
                    up = jnp.where(top, u, pltpu.roll(u, LEV - 1, 1))
                    rhs[turn, f, e] = u + frac * (up - u)
        return 0

    lax.fori_loop(0, rows // UP_ROWS, upstream, 0)
    for keep in keeps:
        keep.wait()


def main_kernel(
    info_ref,
    notes_ref,
    far_low_ref,
    far_high_ref,
    met_ref,
    frac_ref,
    stiff_ref,
    x_ref,
    rhs_in,
    out_any,
    rhs,
    low_kept,
    high_kept,
    ups,
    xa,
    xb,
    nat,
    sems,
    *,
    slots,
):
    lat_rows, cols, width = out_any.shape
    tiles = width // LEV
    rows = lat_rows + NEAR
    wide = cols + 2 * NEAR
    groups = wide // 8
    own0 = jnp.where(info_ref[0] == 0, 0, NEAR)
    ext0 = jnp.where(info_ref[0] == 0, lat_rows, 0)
    keeps = [
        pltpu.make_async_copy(far_low_ref, low_kept, sems.at[tiles]),
        pltpu.make_async_copy(far_high_ref, high_kept, sems.at[tiles + 1]),
    ]
    for keep in keeps:
        keep.start()
    zero = jnp.zeros((8, LEV), jnp.float32)
    for f in range(tiles):
        for k in range(groups):
            xa[f, rows, 8 * k : 8 * k + 8, :] = zero
            xb[f, rows, 8 * k : 8 * k + 8, :] = zero

    def lift(source, ups, count):
        def block(n, _):
            at = pl.ds(pl.multiple_of(n * 8, 8), 8)
            lane = lax.broadcasted_iota(jnp.int32, (8, LEV), 1)
            for f in range(tiles):
                lanes = slice(f * LEV, (f + 1) * LEV)
                u = source[at, lanes]
                ups[at, lanes] = jnp.where(lane == LEV - 1, u, pltpu.roll(u, LEV - 1, 1))
            return 0

        lax.fori_loop(0, count // 8, block, 0)

    def put(side, m, j, n):
        k = 0 if side == 0 else groups - 1
        e = jnp.where(m < lat_rows, own0 + m, ext0 + m - lat_rows)
        column, up = (far_low_ref, far_high_ref)[side][pl.ds(n, 1), :], ups[side, pl.ds(n, 1), :]
        for turn in range(TRAJ):
            hit = met_ref[side, turn, m] == j.astype(jnp.float32)
            frac = frac_ref[m, turn * wide + 8 * k : turn * wide + 8 * k + 8, :]
            for f in range(tiles):
                u, v = column[:, f * LEV : (f + 1) * LEV], up[:, f * LEV : (f + 1) * LEV]
                mixed = u + frac * (v - u)
                at = (turn, f, e, slice(8 * k, 8 * k + 8), slice(None))
                rhs[at] = jnp.where(hit, mixed, rhs[at])

    fars = (far_low_ref, far_high_ref)
    counts = [jnp.minimum(notes_ref[2 + side, LANES - 1], slots) for side in range(2)]
    for side in range(2):
        lift(fars[side], ups.at[side], slots)

    def place(n, _):
        for side in range(2):
            address = notes_ref[4 + side * -(-slots // LANES) + n // LANES, n % LANES]
            put(side, address >> 3, jnp.where(n < counts[side], address & 7, -LANES), n)
        return 0

    lax.fori_loop(0, jnp.maximum(counts[0], counts[1]), place, 0)

    sub = lax.broadcasted_iota(jnp.int32, (8, LEV), 0)
    bottom, last = sub == 0, sub == 7

    def tile(f, _):
        s = stiff_ref[f]
        prev = 1.0
        for sweep in range(2 * TRAJ):
            omega = OMEGAS[sweep % 2]
            alpha = jnp.broadcast_to((1.0 - omega - 4.0 * omega * s) * (prev / omega), (8, LEV))
            beta = jnp.broadcast_to(s * prev, (8, LEV))
            prev = omega
            turn = sweep // 2
            src, dst = (x_ref, xa, xb, xa)[sweep], (xa, xb, xa, None)[sweep]
            beyond = 2 * TRAJ - 1 - sweep
            start = jnp.maximum(own0 - beyond, 0)
            step = max(d for d in range(1, SWEEP_ROWS + 1) if (lat_rows + beyond) % d == 0)

            def load(e, src=src):
                return [src[f, e, 8 * k : 8 * k + 8, :] for k in range(groups)]

            def block(
                group, carry, load=load, dst=dst, alpha=alpha, beta=beta, turn=turn, omega=omega, start=start, step=step
            ):
                south, mid = carry
                for v in range(step):
                    e = start + group * step + v
                    north = load(e + 1)
                    left, right = mid[0], mid[groups - 1]
                    first, final = mid[1], mid[groups - 2]
                    from_west = [pltpu.roll(x, 1, 0) for x in (left, final, right)]
                    from_east = [pltpu.roll(x, 7, 0) for x in (left, first, right)]
                    wests = [from_west[0], jnp.where(bottom, from_west[0], from_west[1])]
                    wests += mid[1 : groups - 2] + [jnp.where(bottom, from_west[1], from_west[2])]
                    easts = [jnp.where(last, from_east[1], from_east[0])] + mid[2 : groups - 1]
                    easts += [jnp.where(last, from_east[2], from_east[1]), from_east[2]]
                    for k in range(groups):
                        around = (south[k] + north[k]) + (wests[k] + easts[k])
                        new = alpha * mid[k] + beta * around + rhs[turn, f, e, 8 * k : 8 * k + 8, :]
                        if dst is not None:
                            dst[f, e, 8 * k : 8 * k + 8, :] = new
                        elif k in (0, groups - 1):
                            nat[f, e, 8 * k : 8 * k + 8, :] = new * omega
                        else:
                            nat[f, e, pl.ds(8 + k - 1, 8, stride=groups - 2), :] = new * omega
                    south, mid = mid, north
                return south, mid

            before = [jnp.where(start == 0, 0.0, v) for v in load(jnp.maximum(start - 1, 0))]
            lax.fori_loop(0, (lat_rows + beyond) // step, block, (before, load(start)))

        lanes = pl.ds(pl.multiple_of(f * LEV, LEV), LEV)
        part = nat.at[f, pl.ds(own0, lat_rows), pl.ds(NEAR, cols), :]
        pltpu.make_async_copy(part, out_any.at[:, :, lanes], sems.at[f]).start()
        return 0

    lax.fori_loop(0, tiles, tile, 0)
    for f in range(tiles):
        part = nat.at[f, pl.ds(own0, lat_rows), pl.ds(NEAR, cols), :]
        pltpu.make_async_copy(part, out_any.at[:, :, pl.ds(f * LEV, LEV)], sems.at[f]).wait()
    for keep in keeps:
        keep.wait()


def shards(state, dep_shift, dep_frac, stiff):
    lat_rows, cols, width = state.shape
    tiles = width // LEV
    rows = lat_rows + NEAR
    wide = cols + 2 * NEAR
    band = cols + 2 * SIDE
    kinds = 2 * TRAJ
    lat = lax.axis_index("lat")
    low = lat == 0
    right, left = ring("lon", 1), ring("lon", -1)
    swap = ring("lat", 1)
    info = lat[None]
    shape = functools.partial(jax.ShapeDtypeStruct, dtype=jnp.float32)
    smem = pl.BlockSpec(memory_space=pltpu.SMEM)
    vmem = pl.BlockSpec(memory_space=pltpu.VMEM)
    anywhere = pl.BlockSpec(memory_space=pl.ANY)
    hbm = pl.BlockSpec(memory_space=pltpu.HBM)

    near = shape((lat_rows * NEAR, width))
    edge, near_left, near_right = pl.pallas_call(
        start_kernel,
        out_shape=(shape((NEAR, cols, width)), near, near),
        in_specs=[smem, hbm],
        out_specs=(vmem,) * 3,
        scratch_shapes=[
            pltpu.VMEM((2, lat_rows, 8, width), jnp.float32),
            pltpu.SemaphoreType.DMA((3,)),
        ],
        compiler_params=pltpu.CompilerParams(vmem_limit_bytes=16 * 2**20),
    )(info, state)
    own = pl.pallas_call(
        turn_kernel,
        out_shape=shape((kinds, cols, LANES)),
        in_specs=[vmem] * 2,
        out_specs=vmem,
        scratch_shapes=[pltpu.VMEM((LANES, LANES), jnp.float32)],
        compiler_params=pltpu.CompilerParams(vmem_limit_bytes=4 * 2**20),
    )(dep_shift, dep_frac)
    other = lax.ppermute(own, "lat", swap)
    edge = lax.ppermute(edge, "lat", swap)
    some = lat_rows // 4 * NEAR
    first = shape((8 + some, width))
    second = shape((rows * NEAR - some, width))
    left_a, right_a, left_b, right_b, dep = pl.pallas_call(
        functools.partial(second_kernel, rows=rows),
        out_shape=(first, first, second, second, shape((kinds, cols, LANES))),
        in_specs=[smem] + [vmem] * 5,
        out_specs=(vmem,) * 5,
        compiler_params=pltpu.CompilerParams(vmem_limit_bytes=4 * 2**20),
    )(info, own, other, edge, near_left, near_right)
    low_a = lax.ppermute(right_a, "lon", right)
    high_a = lax.ppermute(left_a, "lon", left)
    low_b = lax.ppermute(right_b, "lon", right)
    high_b = lax.ppermute(left_b, "lon", left)

    few = shape((SLOTS, width))
    size = rows * 8
    send_low, send_high, notes, over, around = pl.pallas_call(
        functools.partial(pack_kernel, rows=rows, slots=SLOTS),
        out_shape=(
            few,
            few,
            jax.ShapeDtypeStruct((8, LANES), jnp.int32),
            jax.ShapeDtypeStruct((1,), jnp.int32),
            shape((kinds, wide, LANES)),
        ),
        in_specs=[smem] + [vmem] * 5,
        out_specs=(vmem, vmem, vmem, smem, vmem),
        scratch_shapes=[pltpu.SMEM((8, LANES), jnp.int32), pltpu.SemaphoreType.DMA(())],
        compiler_params=pltpu.CompilerParams(vmem_limit_bytes=4 * 2**20),
        cost_estimate=pl.CostEstimate(flops=0, bytes_accessed=40 * 2**20, transcendentals=0),
    )(info, dep, state.reshape(lat_rows * cols, width), edge.reshape(NEAR * cols, width), low_a, high_a)
    far_high = lax.ppermute(send_low, "lon", left)
    far_low = lax.ppermute(send_high, "lon", right)

    per_row = shape((rows, TRAJ * wide, LANES))
    def weights(around):
        return pl.pallas_call(
            functools.partial(weights_kernel, rows=rows),
            out_shape=(per_row, per_row, shape((2, TRAJ, rows, 8, LANES)), shape(around.shape)),
            in_specs=[vmem],
            out_specs=(vmem, vmem, vmem, hbm),
            scratch_shapes=[pltpu.SemaphoreType.DMA(())],
            compiler_params=pltpu.CompilerParams(vmem_limit_bytes=8 * 2**20),
        )(around)

    pick, frac, met, around = weights(around)
    low_b, high_b, pick = lax.optimization_barrier((low_b, high_b, pick))

    rhs_shape = shape((TRAJ, tiles, rows, wide, LEV))
    x_shape = (tiles, rows + 1, wide, LEV)

    def gather(state, edge, low_a, high_a, low_b, high_b, pick, frac):
        return pl.pallas_call(
            gather_kernel,
            out_shape=(rhs_shape, shape(x_shape)) + tuple(shape(x.shape) for x in (edge, low_a, high_a, low_b, high_b)),
            in_specs=[smem, hbm, anywhere] + [vmem] * 6,
            out_specs=(vmem, vmem) + (hbm,) * 5,
            scratch_shapes=[
                pltpu.VMEM((tiles, rows, cols + 2 * SIDE, LEV), jnp.float32),
                pltpu.SemaphoreType.DMA((2 * tiles + 5,)),
            ],
            compiler_params=pltpu.CompilerParams(vmem_limit_bytes=12 * 2**20),
            cost_estimate=pl.CostEstimate(flops=0, bytes_accessed=2**20, transcendentals=0),
        )(info, state, edge, low_a, high_a, low_b, high_b, pick, frac)

    def finish(slots, notes, far_low, far_high, met, frac, x, rhs):
        return pl.pallas_call(
            functools.partial(main_kernel, slots=slots),
            out_shape=(shape(state.shape), rhs_shape, shape(far_low.shape), shape(far_high.shape)),
            in_specs=[smem] * 2 + [vmem] * 7,
            out_specs=(hbm, vmem, hbm, hbm),
            scratch_shapes=[
                pltpu.VMEM((2, slots, width), jnp.float32),
                pltpu.VMEM(x_shape, jnp.float32),
                pltpu.VMEM(x_shape, jnp.float32),
                pltpu.VMEM((tiles, rows, wide, LEV), jnp.float32),
                pltpu.SemaphoreType.DMA((tiles + 2,)),
            ],
            input_output_aliases={8: 1},
            compiler_params=pltpu.CompilerParams(vmem_limit_bytes=16 * 2**20),
        )(info, notes, far_low, far_high, met, frac, stiff.reshape(tiles, 1, LEV), x, rhs)

    rhs, x, *messages = gather(state, edge, low_a, high_a, low_b, high_b, pick, frac)
    out, _, far_low, far_high = finish(SLOTS, notes, far_low, far_high, met, frac, x, rhs)

    def whole():
        counts = notes[:4, LANES - 1]
        most = jnp.maximum(counts[:2], counts[2:])
        over_left, over_right = most[0] > SLOTS, most[1] > SLOTS
        field = jnp.concatenate([state, messages[0]], axis=0)
        at_left = field[:, NEAR : NEAR + 8].reshape(size, width)
        at_right = field[:, cols - NEAR - 8 : cols - NEAR][:, ::-1].reshape(size, width)
        even = lax.axis_index("lon") % 2 == 0
        nothing = jnp.zeros((size, width), jnp.float32)
        got_even = lax.cond(
            jnp.where(even, over_right, over_left),
            lambda: lax.ppermute(jnp.where(even, at_right, at_left), "lon", pairs("lon", 0)),
            lambda: nothing,
        )
        got_odd = lax.cond(
            jnp.where(even, over_left, over_right),
            lambda: lax.ppermute(jnp.where(even, at_left, at_right), "lon", pairs("lon", 1)),
            lambda: nothing,
        )
        lists = -(-size // LANES)
        every = jnp.arange(lists * LANES, dtype=jnp.int32).reshape(lists, LANES)
        more, got = [], []
        for side, (over_side, some) in enumerate(((over_left, far_low), (over_right, far_high))):
            complete = jnp.where((side == 1) == even, got_even, got_odd)
            few = jnp.pad(notes[4 + side : 5 + side], ((0, lists - 1), (0, 0)))
            more.append(jnp.where(over_side, every, few))
            got.append(jnp.where(over_side, complete, jnp.pad(some, ((0, size - SLOTS), (0, 0)))))
        many = jnp.where(jnp.stack([over_left, over_right]), size, counts[2:])
        many = jnp.broadcast_to(jnp.concatenate([counts[:2], many])[:, None], (4, LANES))
        pick, frac, met, _ = weights(around)
        rhs, x, *_ = gather(state, *messages, pick, frac)
        return finish(size, jnp.concatenate([many] + more), got[0], got[1], met, frac, x, rhs)[0]

    return lax.cond(over[0] > 0, whole, lambda: out)


def solution(mesh):
    in_specs = (
        P(("member", "lat"), "lon", None),
        P(None, ("member", "lat"), "lon"),
        P(None, ("member", "lat"), "lon"),
        P(),
    )
    out_specs = P(("member", "lat"), "lon", None)
    return jax.shard_map(shards, mesh=mesh, in_specs=in_specs, out_specs=out_specs, check_vma=False)
```
